256 devices in a mesh: ctx: 32 (over y, z), kvh: 8 (over x, core).
Axes of the slice: x: 4, y: 4, z: 8, core: 2. Of those that a mesh axis runs over, the one named last changes fastest.
Arguments:
- front_hidden: bfloat16 [8192, 4096], P('ctx', 'kvh'), may hold values from -6 to 6
- norm_gain: bfloat16 [4096], replicated, may hold values from 0.099609375 to 1.8984375
- w_qkv: bfloat16 [4096, 6144], P(None, 'kvh')
- block_span: int32 [32], replicated, may hold values from 0 to 31, each once
- back_pages: bfloat16 [8192, 8, 2, 16, 128], P('ctx', 'kvh'), may hold values from -6 to 6
- page_dest: int32 [8192], P('ctx'), may hold values from -1 to 31, as said below
Outputs:
- attn_out: bfloat16 [8192, 4096], P('ctx', 'kvh')
- front_cache: bfloat16 [8192, 8, 256], P('ctx', 'kvh')
- restored_pages: bfloat16 [8192, 8, 2, 16, 128], P('ctx', 'kvh')
- page_count: int32 [32], P('ctx')
The draws below stay inside these ranges and needn't reach their ends.
Inputs may be any that keep to these rules, and one draw needn't show every extreme that they name: `block_span`: a permutation of the span numbers. `page_dest`: the slots of one store name each owner at most 8 times, and some store names some owner exactly 8 times; every owner receives at most 256 pages over all stores, and some owner exactly 256.
All inputs are finite; a program needn't handle non-finite values.
Results may differ from the reference program's by a relative error of at most 0.008.
The reference program's roundings to bfloat16 on the way count: a program that leaves them out, or rounds other values in their place, can miss the bound.
Values may be sent and summed in bfloat16 or wider, within the bound.
No kernel may reach another device: no remote copies, remote signals or barrier semaphores. Data moves between devices by JAX's collectives and lax.ppermute only.
A program may use at most 64 MiB of HBM per device.

```python
import jax
import jax.numpy as jnp
from jax import lax

D = 4096
HD = 128
GQ = 4
KVH = 8
QH = 32
SPAN = 256
FRONT = 8192
PAGE = 16
SEND_CAP = 8
PAGES_DEV = 256
PAGES = 8192
OWN_CAP = 256
N_CTX = 32


def draw_w_qkv(key, part):
    key = jax.random.fold_in(key, 5)
    base = jax.random.normal(key, (D, KVH, GQ + 2, HD), jnp.float32) * D ** (-0.5)
    return base.reshape(D, KVH * (GQ + 2) * HD).astype(jnp.bfloat16)


def draw_page_dest(key, part):
    key = jax.random.fold_in(key, 9)
    key_counts, key_full, key_shuffle = jax.random.split(key, 3)
    owner_total = PAGES_DEV // SEND_CAP
    counts = jax.random.randint(key_counts, (owner_total, owner_total), 1, SEND_CAP + 1)
    full_owner = jax.random.randint(key_full, (), 0, owner_total)
    owner_iota = jnp.arange(owner_total)
    counts = jnp.where(owner_iota[None, :] == full_owner, SEND_CAP, counts)
    slot_iota = jnp.arange(PAGES_DEV)
    owner_of = slot_iota // SEND_CAP
    within = slot_iota % SEND_CAP
    live = within[None, :] < counts[:, owner_of]
    dest_map = jnp.where(live, owner_of[None, :], -1)
    shuffles = jax.vmap(lambda subkey: jax.random.permutation(subkey, PAGES_DEV))(jax.random.split(key_shuffle, owner_total))
    dest_map = jnp.take_along_axis(dest_map, shuffles, axis=1)
    return dest_map.reshape(-1).astype(jnp.int32)


def shard_levels(key, extent, cuts, least, top_value):
    loudness = 1.0
    for axis_at, parts in cuts:
        draws = jax.random.uniform(jax.random.fold_in(jax.random.fold_in(key, 6), axis_at), (parts,), jnp.float32, least / len(cuts), top_value / len(cuts))
        loudness = loudness * jnp.repeat(jnp.exp(draws), extent[axis_at] // parts).reshape((-1,) + (1,) * (len(extent) - 1 - axis_at))
    return loudness


def gaussian(own_key, dims, spread, most, cuts=(), held_as=jnp.bfloat16):
    entries = spread * jax.random.normal(own_key, dims, jnp.float32)
    if cuts:
        entries = entries * shard_levels(own_key, dims, cuts, -0.22, 0.18)
    return jnp.clip(entries, -most, most).astype(held_as)


def setup_inputs(seed: int = 0) -> dict:
    arg_keys = jax.random.split(jax.random.key(seed), 7)
    front_hidden = gaussian(arg_keys[0], (FRONT, D), 1.0, 6.0, ((0, 32), (1, 8)))
    norm_gain = jnp.clip(1.0 + 0.18 * jax.random.normal(arg_keys[1], (D,), jnp.float32), 0.099609375, 1.8984375).astype(jnp.bfloat16)
    w_qkv = draw_w_qkv(jax.random.fold_in(arg_keys[6], 71), 0)
    block_span = jax.random.permutation(arg_keys[3], N_CTX).astype(jnp.int32)
    back_pages = gaussian(arg_keys[4], (PAGES, KVH, 2, PAGE, HD), 1.0, 6.0, ((0, 32), (1, 8)))
    page_dest = draw_page_dest(jax.random.fold_in(arg_keys[6], 71), 0)
    return {"front_hidden": front_hidden, "norm_gain": norm_gain, "w_qkv": w_qkv, "block_span": block_span, "back_pages": back_pages, "page_dest": page_dest}


ROPE_BASE = 500000.0

def rotate(vectors, positions):
    half_dim = HD // 2
    inv_freq = ROPE_BASE ** (-(2 * jnp.arange(half_dim)).astype(jnp.float32) / HD)
    angles = positions.astype(jnp.float32)[:, None] * inv_freq[None, :]
    cosine = jnp.cos(angles)[:, None, :]
    sine = jnp.sin(angles)[:, None, :]
    first = vectors[..., :half_dim]
    second = vectors[..., half_dim:]
    return jnp.concatenate([first * cosine - second * sine, second * cosine + first * sine], axis=-1)

def reference(front_hidden, norm_gain, w_qkv, block_span, back_pages, page_dest):
    widened = front_hidden.astype(jnp.float32)
    mean_sq = lax.optimization_barrier(jnp.mean(widened * widened, axis=-1, keepdims=True))
    normed = (widened * lax.rsqrt(mean_sq + 1e-05) * norm_gain.astype(jnp.float32)).astype(jnp.bfloat16)
    projected = jnp.dot(normed, w_qkv, preferred_element_type=jnp.float32).reshape(FRONT, KVH, GQ + 2, HD)
    row_iota = jnp.arange(FRONT).astype(jnp.int32)
    positions = block_span[row_iota // SPAN] * SPAN + row_iota % SPAN
    queries = rotate(projected[:, :, :GQ].reshape(FRONT, KVH * GQ, HD), positions).astype(jnp.bfloat16)
    key_rows = rotate(projected[:, :, GQ], positions).astype(jnp.bfloat16)
    value_rows = projected[:, :, GQ + 1].astype(jnp.bfloat16)
    front_cache = jnp.concatenate([key_rows, value_rows], axis=-1)
    holder = jnp.argsort(block_span).astype(jnp.int32)
    order = (holder[:, None] * SPAN + jnp.arange(SPAN).astype(jnp.int32)[None, :]).reshape(-1)
    sorted_q = queries[order].reshape(FRONT, KVH, GQ, HD).astype(jnp.float32)
    sorted_k = key_rows[order].astype(jnp.float32)
    sorted_v = value_rows[order].astype(jnp.float32)
    pieces = []
    for block in range(N_CTX):
        row_start = block * SPAN
        row_end = row_start + SPAN
        query_block = sorted_q[row_start:row_end]
        scores = jnp.einsum('qhgd,khd->hgqk', query_block, sorted_k[:row_end]) * HD ** (-0.5)
        query_pos = jnp.arange(row_start, row_end)
        key_pos = jnp.arange(row_end)
        allowed = key_pos[None, :] <= query_pos[:, None]
        scores = jnp.where(allowed, scores, -jnp.inf)
        top = lax.optimization_barrier(jnp.max(scores, axis=-1, keepdims=True))
        weights = jnp.exp(scores - top)
        totals = lax.optimization_barrier(jnp.sum(weights, axis=-1))
        rounded = lax.optimization_barrier(weights.astype(jnp.bfloat16)).astype(jnp.float32)
        context = jnp.einsum('hgqk,khd->qhgd', rounded, sorted_v[:row_end])
        context = context / jnp.transpose(totals, (2, 0, 1))[..., None]
        pieces.append(context.reshape(SPAN, QH * HD))
    sorted_out = jnp.concatenate(pieces, axis=0).astype(jnp.bfloat16)
    attn_out = jnp.zeros((FRONT, QH * HD), jnp.bfloat16).at[order].set(sorted_out)
    owner_iota = jnp.arange(N_CTX).astype(jnp.int32)
    onehot = (page_dest[:, None] == owner_iota[None, :]).astype(jnp.int32)
    rank = lax.optimization_barrier(jnp.sum((jnp.cumsum(onehot, axis=0) - onehot) * onehot, axis=1))
    slot = jnp.where(page_dest >= 0, page_dest * OWN_CAP + rank, N_CTX * OWN_CAP).astype(jnp.int32)
    restored_pages = jnp.zeros((N_CTX * OWN_CAP, KVH, 2, PAGE, HD), jnp.bfloat16).at[slot].set(back_pages, mode='drop')
    page_count = lax.optimization_barrier(jnp.sum(onehot, axis=0)).astype(jnp.int32)
    return (attn_out, front_cache, restored_pages, page_count)
```

```python
import jax
import jax.numpy as jnp
from jax import lax
from jax.experimental import pallas as pl
from jax.experimental.pallas import tpu as pltpu
from jax.sharding import PartitionSpec as P

HD = 128
GQ = 4
SPAN = 256
SEND_CAP = 8
NY = 4
NZ = 8
N_CTX = NY * NZ
OWN_CAP = N_CTX * SEND_CAP
D = 4096
ROWS = GQ * SPAN
PAGE_ROWS = 32
ROPE_BASE = 500000.0
MASK_FILL = -1e30
SCALE_LOG2 = HD**-0.5 * 1.4426950408889634
MARK = 64.0
STATS = 16

VMEM = pl.BlockSpec(memory_space=pltpu.VMEM)
SMEM = pl.BlockSpec(memory_space=pltpu.SMEM)
ANY = pl.BlockSpec(memory_space=pl.ANY)


def params(mib):
    return pltpu.CompilerParams(vmem_limit_bytes=mib * 2**20)


def bucket_kernel(dest_ref, pages_ref, out_ref, count_ref):
    for owner in range(N_CTX):
        count_ref[owner] = 0

    def put(page, carry):
        owner = dest_ref[page]

        @pl.when(owner >= 0)
        def _():
            rank = count_ref[owner]
            count_ref[owner] = rank + 1
            out_ref[owner * SEND_CAP + rank] = pages_ref[page]

        return carry

    lax.fori_loop(0, OWN_CAP, put, 0, unroll=8)

    def mark(owner, carry):
        count = count_ref[owner]

        @pl.when(count < SEND_CAP)
        def _():
            value = jnp.full((16, HD), MARK + count.astype(jnp.float32), jnp.float32)
            out_ref[owner * SEND_CAP + SEND_CAP - 1, 0:16, :] = value.astype(jnp.bfloat16)

        return carry

    lax.fori_loop(0, N_CTX, mark, 0)


def bucket(page_dest, pages):
    return pl.pallas_call(
        bucket_kernel,
        out_shape=jax.ShapeDtypeStruct((OWN_CAP, PAGE_ROWS, HD), jnp.bfloat16),
        in_specs=[SMEM, VMEM],
        out_specs=VMEM,
        scratch_shapes=[pltpu.SMEM((N_CTX,), jnp.int32)],
        compiler_params=params(16),
        name="bucket",
    )(page_dest, pages)


def place_kernel(arrived_ref, out_ref, total_ref, placed_ref, sem):
    offset = jnp.int32(0)
    for store in range(N_CTX):
        last = arrived_ref[store * SEND_CAP + SEND_CAP - 1, 0:16, :].astype(jnp.float32)
        top = jnp.max(last)
        count = jnp.where(top > MARK / 2, (top - MARK).astype(jnp.int32), SEND_CAP)
        for rank in range(SEND_CAP):
            placed_ref[offset + rank] = arrived_ref[store * SEND_CAP + rank]
        offset = offset + count
    total_ref[0] = offset

    def clear(page, carry):
        placed_ref[page] = jnp.zeros((PAGE_ROWS, HD), jnp.bfloat16)
        return carry

    lax.fori_loop(offset, OWN_CAP, clear, 0)
    copy = pltpu.make_async_copy(placed_ref.at[pl.ds(0, OWN_CAP)], out_ref, sem)
    copy.start()
    copy.wait()


def place(arrived):
    return pl.pallas_call(
        place_kernel,
        out_shape=(
            jax.ShapeDtypeStruct((OWN_CAP, PAGE_ROWS, HD), jnp.bfloat16),
            jax.ShapeDtypeStruct((1,), jnp.int32),
        ),
        in_specs=[VMEM],
        out_specs=(ANY, SMEM),
        scratch_shapes=[
            pltpu.VMEM((OWN_CAP + SEND_CAP, PAGE_ROWS, HD), jnp.bfloat16),
            pltpu.SemaphoreType.DMA,
        ],
        compiler_params=params(16),
        name="place",
    )(arrived)


def project_kernel(index_ref, gain_ref, cos_ref, sin_ref, w_ref, *refs):
    blocks = refs[:8]
    qt_ref, cache_ref, msg_ref, normed_ref = refs[8:]
    width = blocks[0].shape[1]
    squares = jnp.zeros((SPAN, HD), jnp.float32)
    for block in blocks:
        for at in range(0, width, HD):
            part = block[:, at : at + HD].astype(jnp.float32)
            squares = squares + part * part
    inverse = lax.rsqrt(jnp.sum(squares, axis=1, keepdims=True) * (1.0 / D) + 1e-05)
    for number, block in enumerate(blocks):
        index = index_ref[number]
        gain = gain_ref[pl.ds(index, 1), :]
        normed = block[...].astype(jnp.float32) * inverse * gain
        start = pl.multiple_of(index * width, width)
        normed_ref[:, pl.ds(start, width)] = normed.astype(jnp.bfloat16)
    projected = jnp.dot(normed_ref[...], w_ref[...], preferred_element_type=jnp.float32)
    cosine = cos_ref[...]
    sine = sin_ref[...]

    def rope(u):
        return u * cosine + pltpu.roll(u, HD // 2, 1) * sine

    for head in range(GQ):
        turned = rope(projected[:, head * HD : (head + 1) * HD])
        qt_ref[:, head * SPAN : (head + 1) * SPAN] = turned.T.astype(jnp.bfloat16)
    key = rope(projected[:, GQ * HD : (GQ + 1) * HD]).astype(jnp.bfloat16)
    value = projected[:, (GQ + 1) * HD :]
    cache_ref[:, :HD] = key
    cache_ref[:, HD:] = value.astype(jnp.bfloat16)
    msg_ref[:, :HD] = key
    for at in (0, HD):
        msg_ref[at : at + HD, HD:] = value[at : at + HD].T.astype(jnp.bfloat16)


def project(index, gain, cosine, sine, w_qkv, blocks):
    return pl.pallas_call(
        project_kernel,
        out_shape=(
            jax.ShapeDtypeStruct((HD, ROWS), jnp.bfloat16),
            jax.ShapeDtypeStruct((SPAN, 2 * HD), jnp.bfloat16),
            jax.ShapeDtypeStruct((SPAN, 2 * HD), jnp.bfloat16),
        ),
        in_specs=[SMEM] + [VMEM] * 12,
        out_specs=(VMEM, VMEM, VMEM),
        scratch_shapes=[pltpu.VMEM((SPAN, D), jnp.bfloat16)],
        compiler_params=params(32),
        name="project",
    )(index, gain, cosine, sine, w_qkv, *blocks)


def attend_kernel(qspan_ref, kspan_ref, *refs):
    queries = refs[:NY]
    messages = refs[NY : NY + NZ]
    outs = refs[NY + NZ : 2 * NY + NZ]
    kv_ref, acc_ref, max_ref, sum_ref = refs[2 * NY + NZ :]
    for number, message in enumerate(messages):
        kv_ref[number] = message[...]
    key_at = lax.broadcasted_iota(jnp.int32, (SPAN, SPAN), 0)
    query_at = lax.broadcasted_iota(jnp.int32, (SPAN, SPAN), 1)

    for number in range(NY):
        query_ref = queries[number]
        query_span = qspan_ref[number]
        acc_ref[...] = jnp.zeros_like(acc_ref)
        max_ref[...] = jnp.full_like(max_ref, MASK_FILL)
        sum_ref[...] = jnp.zeros_like(sum_ref)

        def update(part, masked):
            key = kv_ref[part, :, :HD]
            value = kv_ref[part, :, HD:]
            value = jnp.concatenate([value[:HD], value[HD:]], axis=1)
            for head in range(GQ):
                lanes = slice(head * SPAN, (head + 1) * SPAN)
                scores = jnp.dot(key, query_ref[:, lanes], preferred_element_type=jnp.float32)
                if masked:
                    scores = jnp.where(key_at <= query_at, scores, MASK_FILL)
                old_max = max_ref[:, lanes]
                new_max = jnp.maximum(old_max, jnp.max(scores, axis=0, keepdims=True))
                weights = jnp.exp2((scores - new_max) * SCALE_LOG2)
                fade = jnp.exp2((old_max - new_max) * SCALE_LOG2)
                sum_ref[:, lanes] = sum_ref[:, lanes] * fade + jnp.sum(weights, axis=0, keepdims=True)
                product = jnp.dot(
                    value, weights.astype(jnp.bfloat16), preferred_element_type=jnp.float32
                )
                acc_ref[:, lanes] = acc_ref[:, lanes] * fade + product
                max_ref[:, lanes] = new_max

        def step(part, carry):
            key_span = kspan_ref[part]

            @pl.when(key_span < query_span)
            def _():
                update(part, False)

            @pl.when(key_span == query_span)
            def _():
                update(part, True)

            return carry

        lax.fori_loop(0, NZ, step, 0)
        total = jnp.maximum(sum_ref[...], 1.0)
        outs[number][:HD, :] = (acc_ref[...] / total).astype(jnp.bfloat16)
        level = max_ref[...] * SCALE_LOG2 + jnp.log2(total)
        high = level.astype(jnp.bfloat16).astype(jnp.float32)
        middle = (level - high).astype(jnp.bfloat16).astype(jnp.float32)
        low = level - high - middle
        row = lax.broadcasted_iota(jnp.int32, (STATS, ROWS), 0)
        stats = jnp.where(row == 0, high, jnp.where(row == 1, middle, jnp.where(row == 2, low, 0.0)))
        outs[number][HD:, :] = stats.astype(jnp.bfloat16)


def attend(query_spans, key_spans, queries, messages):
    part = jax.ShapeDtypeStruct((HD + STATS, ROWS), jnp.bfloat16)
    return pl.pallas_call(
        attend_kernel,
        out_shape=(part,) * NY,
        in_specs=[SMEM, SMEM] + [VMEM] * (NY + NZ),
        out_specs=(VMEM,) * NY,
        scratch_shapes=[
            pltpu.VMEM((NZ, SPAN, 2 * HD), jnp.bfloat16),
            pltpu.VMEM((HD, ROWS), jnp.float32),
            pltpu.VMEM((1, ROWS), jnp.float32),
            pltpu.VMEM((1, ROWS), jnp.float32),
        ],
        compiler_params=params(32),
        name="attend",
    )(query_spans, key_spans, *queries, *messages)


def merge_kernel(*refs):
    parts, out_ref = refs[:NY], refs[NY]
    levels = []
    for part in parts:
        stats = part[HD:, :].astype(jnp.float32)
        levels.append(stats[0:1] + stats[1:2] + stats[2:3])
    top = levels[0]
    for level in levels[1:]:
        top = jnp.maximum(top, level)
    weights = [jnp.exp2(level - top) for level in levels]
    total = weights[0]
    for weight in weights[1:]:
        total = total + weight
    for head in range(GQ):
        lanes = slice(head * SPAN, (head + 1) * SPAN)
        context = jnp.zeros((HD, SPAN), jnp.float32)
        for part, weight in zip(parts, weights):
            context = context + part[:HD, lanes].astype(jnp.float32) * weight[:, lanes]
        context = context / total[:, lanes]
        out_ref[:, head * HD : (head + 1) * HD] = context.T.astype(jnp.bfloat16)


def merge(parts):
    return pl.pallas_call(
        merge_kernel,
        out_shape=jax.ShapeDtypeStruct((SPAN, GQ * HD), jnp.bfloat16),
        in_specs=[VMEM] * NY,
        out_specs=VMEM,
        compiler_params=params(16),
        name="merge",
    )(*parts)


def rotation(positions):
    half_dim = HD // 2
    inv_freq = ROPE_BASE ** (-(2 * jnp.arange(half_dim)).astype(jnp.float32) / HD)
    angles = positions.astype(jnp.float32)[:, None] * inv_freq[None, :]
    cosine = jnp.cos(angles)
    sine = jnp.sin(angles)
    return jnp.concatenate([cosine, cosine], axis=1), jnp.concatenate([-sine, sine], axis=1)


def along_x(value, step):
    return lax.ppermute(value, "kvh", [(i, ((i // 2 + step) % 4) * 2 + i % 2) for i in range(8)])


def across(value):
    return lax.ppermute(value, "kvh", [(i, i ^ 1) for i in range(8)])


def along_y(value, step):
    return lax.ppermute(
        value, "ctx", [(i, ((i // NZ + step) % NY) * NZ + i % NZ) for i in range(N_CTX)]
    )


def along_z(value, step):
    return lax.ppermute(
        value, "ctx", [(i, (i // NZ) * NZ + (i % NZ + step) % NZ) for i in range(N_CTX)]
    )


def shards(front_hidden, norm_gain, w_qkv, block_span, back_pages, page_dest):
    my_index = lax.axis_index("ctx")
    my_y, my_z = my_index // NZ, my_index % NZ
    my_kvh = lax.axis_index("kvh")
    my_x, my_core = my_kvh // 2, my_kvh % 2

    steps_x = (0, 1, 3, 2)
    same = [front_hidden] + [along_x(front_hidden, step) for step in steps_x[1:]]
    other = [across(block) for block in same]
    sources = [(my_x - step) % 4 for step in steps_x]
    index = jnp.stack(
        [source * 2 + my_core for source in sources]
        + [source * 2 + 1 - my_core for source in sources]
    ).astype(jnp.int32)

    pages = back_pages.reshape(OWN_CAP, PAGE_ROWS, HD)
    outgoing = bucket(page_dest, pages).reshape(N_CTX, SEND_CAP, PAGE_ROWS, HD)
    arrived = lax.all_to_all(outgoing, "ctx", split_axis=0, concat_axis=0, tiled=True)

    positions = block_span[my_index] * SPAN + jnp.arange(SPAN)
    cosine, sine = rotation(positions)
    gain = norm_gain.astype(jnp.float32).reshape(8, D // 8)
    query, cache, message = project(index, gain, cosine, sine, w_qkv, same + other)

    up, down = [message], [message]
    for _ in range(3):
        up.append(along_z(up[-1], 1))
        down.append(along_z(down[-1], -1))
    down.append(along_z(down[-1], -1))
    messages = up + down[1:]
    key_steps = [0, -1, -2, -3, 1, 2, 3, 4]
    key_spans = jnp.stack([block_span[my_y * NZ + (my_z + step) % NZ] for step in key_steps])

    from_up = along_y(query, -1)
    queries = [query, along_y(query, 1), from_up, along_y(from_up, -1)]
    query_steps = [0, -1, 1, 2]
    query_spans = jnp.stack([block_span[((my_y + step) % NY) * NZ + my_z] for step in query_steps])

    parts = attend(query_spans, key_spans, queries, messages)
    back = [along_y(part, step) for part, step in zip(parts[1:], query_steps[1:])]
    attn_out = merge([parts[0]] + back)

    restored, page_count = place(arrived.reshape(OWN_CAP, PAGE_ROWS, HD))
    return (
        attn_out,
        cache.reshape(SPAN, 1, 2 * HD),
        restored.reshape(back_pages.shape),
        page_count,
    )


def solution(mesh):
    placed = (
        P("ctx", "kvh"),
        P(),
        P(None, "kvh"),
        P(),
        P("ctx", "kvh", None, None, None),
        P("ctx"),
    )
    return jax.shard_map(
        shards,
        mesh=mesh,
        in_specs=placed,
        out_specs=(
            P("ctx", "kvh"),
            P("ctx", "kvh", None),
            P("ctx", "kvh", None, None, None),
            P("ctx"),
        ),
        check_vma=False,
    )
```

```python
import functools

import jax
import jax.numpy as jnp
from jax import lax
from jax.experimental import pallas as pl
from jax.experimental.pallas import tpu as pltpu
from jax.sharding import PartitionSpec as P

HD = 128
GQ = 4
SPAN = 256
SEND_CAP = 8
NY = 4
NZ = 8
N_CTX = NY * NZ
OWN_CAP = N_CTX * SEND_CAP
FIRST = 3
SECOND = SEND_CAP - FIRST
D = 4096
ROWS = GQ * SPAN
PAGE_ROWS = 32
ROPE_BASE = 500000.0
MASK_FILL = -1e30
SCALE_LOG2 = HD**-0.5 * 1.4426950408889634
MARK = 64.0
STATS = 16
STEPS_X = (0, 1, 3, 2)
STEPS_Y = (0, -1, 1, 2)
STEPS_Z = (0, -1, -2, -3, 1, 2, 3, 4)

VMEM = pl.BlockSpec(memory_space=pltpu.VMEM)
SMEM = pl.BlockSpec(memory_space=pltpu.SMEM)
HBM = pl.BlockSpec(memory_space=pltpu.HBM)


def params(mib):
    return pltpu.CompilerParams(vmem_limit_bytes=mib * 2**20)


def cost(mib):
    return pl.CostEstimate(flops=0, bytes_accessed=mib * 2**20, transcendentals=0)


def bucket_kernel(dest_hbm, pages_hbm, first_out, second_out, *refs):
    dest_ref, pages_ref, held_ref, count_ref, in_sems, sems = refs
    loads = [
        pltpu.make_async_copy(dest_hbm, dest_ref, in_sems.at[0]),
        pltpu.make_async_copy(pages_hbm, pages_ref, in_sems.at[1]),
    ]
    for load in loads:
        load.start()
    for owner in range(N_CTX + 1):
        count_ref[owner] = 0
    for load in loads:
        load.wait()

    def put(page, carry):
        owner = dest_ref[page]
        held = owner >= 0
        entry = jnp.where(held, owner, N_CTX)
        rank = count_ref[entry]
        count_ref[entry] = rank + 1
        held_ref[entry, jnp.where(held, rank, 0)] = pages_ref[page]
        return carry

    lax.fori_loop(0, OWN_CAP, put, 0, unroll=16)

    for entry in range(N_CTX):
        count = count_ref[entry]
        value = jnp.full((16, HD), MARK + count.astype(jnp.float32), jnp.float32)
        here = held_ref[entry, SEND_CAP - 1, 0:16, :]
        marked = jnp.where(count < SEND_CAP, value.astype(jnp.bfloat16), here)
        held_ref[entry, SEND_CAP - 1, 0:16, :] = marked
    buckets = held_ref.at[pl.ds(0, N_CTX)]
    copies = [
        pltpu.make_async_copy(buckets.at[:, pl.ds(0, FIRST)], first_out, sems.at[0]),
        pltpu.make_async_copy(buckets.at[:, pl.ds(FIRST, SECOND)], second_out, sems.at[1]),
    ]
    for copy in copies:
        copy.start()
    for copy in copies:
        copy.wait()


def bucket(page_dest, pages):
    return pl.pallas_call(
        bucket_kernel,
        out_shape=tuple(
            jax.ShapeDtypeStruct((N_CTX, n, PAGE_ROWS, HD), jnp.bfloat16) for n in (FIRST, SECOND)
        ),
        in_specs=[HBM, HBM],
        out_specs=(HBM, HBM),
        scratch_shapes=[
            pltpu.SMEM((OWN_CAP,), jnp.int32),
            pltpu.VMEM((OWN_CAP, PAGE_ROWS, HD), jnp.bfloat16),
            pltpu.VMEM((N_CTX + 1, SEND_CAP, PAGE_ROWS, HD), jnp.bfloat16),
            pltpu.SMEM((N_CTX + 1,), jnp.int32),
            pltpu.SemaphoreType.DMA((2,)),
            pltpu.SemaphoreType.DMA((2,)),
        ],
        compiler_params=params(56),
        cost_estimate=cost(18),
        name="bucket",
    )(page_dest, pages)


def place_kernel(first_ref, second_ref, out_ref, total_ref, held_ref, placed_ref, sems):
    copies = [
        pltpu.make_async_copy(first_ref, held_ref.at[:, pl.ds(0, FIRST)], sems.at[0]),
        pltpu.make_async_copy(second_ref, held_ref.at[:, pl.ds(FIRST, SECOND)], sems.at[1]),
    ]
    for copy in copies:
        copy.start()
    for copy in copies:
        copy.wait()
    offset = jnp.int32(0)
    for store in range(N_CTX):
        last = held_ref[store, SEND_CAP - 1, 0:16, :].astype(jnp.float32)
        top = jnp.max(last)
        count = jnp.where(top > MARK / 2, (top - MARK).astype(jnp.int32), SEND_CAP)
        for rank in range(SEND_CAP):
            placed_ref[offset + rank] = held_ref[store, rank]
        offset = offset + count
    total_ref[0] = offset

    def clear(page, carry):
        placed_ref[page] = jnp.zeros((PAGE_ROWS, HD), jnp.bfloat16)
        return carry

    lax.fori_loop(offset, OWN_CAP, clear, 0)
    copy = pltpu.make_async_copy(placed_ref.at[pl.ds(0, OWN_CAP)], out_ref, sems.at[0])
    copy.start()
    copy.wait()


def place(first, second):
    return pl.pallas_call(
        place_kernel,
        out_shape=(
            jax.ShapeDtypeStruct((OWN_CAP, PAGE_ROWS, HD), jnp.bfloat16),
            jax.ShapeDtypeStruct((1,), jnp.int32),
        ),
        in_specs=[HBM, HBM],
        out_specs=(HBM, SMEM),
        scratch_shapes=[
            pltpu.VMEM((N_CTX, SEND_CAP, PAGE_ROWS, HD), jnp.bfloat16),
            pltpu.VMEM((OWN_CAP + SEND_CAP, PAGE_ROWS, HD), jnp.bfloat16),
            pltpu.SemaphoreType.DMA((2,)),
        ],
        compiler_params=params(16),
        cost_estimate=cost(10),
        name="place",
    )(first, second)


def project_kernel(gain_ref, cos_ref, sin_ref, w_hbm, *refs):
    blocks = refs[:8]
    qt_ref, cache_ref, msg_ref, w_ref, normed_ref, sems = refs[8:]
    width = blocks[0].shape[1]
    loads = [
        pltpu.make_async_copy(
            w_hbm.at[pl.ds(at * width, width)], w_ref.at[pl.ds(at * width, width)], sems.at[at]
        )
        for at in range(8)
    ]
    for load in loads:
        load.start()
    squares = jnp.zeros((SPAN, HD), jnp.float32)
    for block in blocks:
        for at in range(0, width, HD):
            part = block[:, at : at + HD].astype(jnp.float32)
            squares = squares + part * part
    inverse = lax.rsqrt(jnp.sum(squares, axis=1, keepdims=True) * (1.0 / D) + 1e-05)
    my_kvh = lax.axis_index("kvh")
    my_x, my_core = my_kvh // 2, my_kvh % 2
    for number, block in enumerate(blocks):
        source = (my_x - STEPS_X[number % 4]) & 3
        index = source * 2 + (my_core if number < 4 else 1 - my_core)
        gain = gain_ref[pl.ds(index, 1), :]
        normed = block[...].astype(jnp.float32) * inverse * gain
        start = pl.multiple_of(index * width, width)
        normed_ref[:, pl.ds(start, width)] = normed.astype(jnp.bfloat16)
    for load in loads:
        load.wait()
    projected = jnp.dot(normed_ref[...], w_ref[...], preferred_element_type=jnp.float32)
    cosine = cos_ref[...]
    sine = sin_ref[...]

    def rope(u):
        return u * cosine + pltpu.roll(u, HD // 2, 1) * sine

    for head in range(GQ):
        turned = rope(projected[:, head * HD : (head + 1) * HD])
        qt_ref[:, head * SPAN : (head + 1) * SPAN] = turned.T.astype(jnp.bfloat16)
    key = rope(projected[:, GQ * HD : (GQ + 1) * HD]).astype(jnp.bfloat16)
    value = projected[:, (GQ + 1) * HD :]
    cache_ref[:, :HD] = key
    cache_ref[:, HD:] = value.astype(jnp.bfloat16)
    msg_ref[:, :HD] = key
    for at in (0, HD):
        msg_ref[at : at + HD, HD:] = value[at : at + HD].T.astype(jnp.bfloat16)


def project(gain, cosine, sine, w_qkv, blocks):
    return pl.pallas_call(
        project_kernel,
        out_shape=(
            jax.ShapeDtypeStruct((HD, ROWS), jnp.bfloat16),
            jax.ShapeDtypeStruct((SPAN, 2 * HD), jnp.bfloat16),
            jax.ShapeDtypeStruct((SPAN, 2 * HD), jnp.bfloat16),
        ),
        in_specs=[VMEM] * 3 + [HBM] + [VMEM] * 8,
        out_specs=(VMEM, VMEM, VMEM),
        scratch_shapes=[
            pltpu.VMEM(w_qkv.shape, jnp.bfloat16),
            pltpu.VMEM((SPAN, D), jnp.bfloat16),
            pltpu.SemaphoreType.DMA((8,)),
        ],
        compiler_params=params(56),
        cost_estimate=cost(16),
        name="project",
    )(gain, cosine, sine, w_qkv, *blocks)


def attend_kernel(steps, span_ref, *refs):
    size = len(steps)
    queries = refs[:size]
    messages = refs[size : size + NZ]
    outs = refs[size + NZ : 2 * size + NZ]
    kv_ref, acc_ref, max_ref, sum_ref, list_ref = refs[2 * size + NZ :]
    my_index = lax.axis_index("ctx")
    my_y, my_z = my_index // NZ, my_index % NZ
    for number, message in enumerate(messages):
        kv_ref[number] = message[...]
    key_at = lax.broadcasted_iota(jnp.int32, (SPAN, SPAN), 0)
    query_at = lax.broadcasted_iota(jnp.int32, (SPAN, SPAN), 1)
    heads = [slice(head * SPAN, (head + 1) * SPAN) for head in range(GQ)]
    key_spans = [span_ref[my_y * NZ + ((my_z + step) & (NZ - 1))] for step in STEPS_Z]

    for number, away in enumerate(steps):
        query_ref = queries[number]
        query_span = span_ref[((my_y + away) & (NY - 1)) * NZ + my_z]
        acc_ref[...] = jnp.zeros_like(acc_ref)
        max_ref[...] = jnp.full_like(max_ref, MASK_FILL)
        sum_ref[...] = jnp.zeros_like(sum_ref)

        def update(parts, masked):
            keys, values = [], []
            for part in parts:
                keys.append(kv_ref[part, :, :HD])
                value = kv_ref[part, :, HD:]
                values += [value[:HD], value[HD:]]
            key = jnp.concatenate(keys, axis=0)
            value = jnp.concatenate(values, axis=1)
            scores = [
                jnp.dot(key, query_ref[:, lanes], preferred_element_type=jnp.float32)
                for lanes in heads
            ]
            if masked:
                scores = [jnp.where(key_at <= query_at, score, MASK_FILL) for score in scores]
            old = [max_ref[:, lanes] for lanes in heads]
            new = [
                jnp.maximum(top, jnp.max(score, axis=0, keepdims=True))
                for top, score in zip(old, scores)
            ]
            weights = [jnp.exp2((score - top) * SCALE_LOG2) for score, top in zip(scores, new)]
            fades = [jnp.exp2((before - top) * SCALE_LOG2) for before, top in zip(old, new)]
            products = [
                jnp.dot(value, weight.astype(jnp.bfloat16), preferred_element_type=jnp.float32)
                for weight in weights
            ]
            for head, lanes in enumerate(heads):
                total = jnp.sum(weights[head], axis=0, keepdims=True)
                sum_ref[:, lanes] = sum_ref[:, lanes] * fades[head] + total
                acc_ref[:, lanes] = acc_ref[:, lanes] * fades[head] + products[head]
                max_ref[:, lanes] = new[head]

        earlier = jnp.int32(0)
        for part, key_span in enumerate(key_spans):
            list_ref[earlier] = part
            earlier = earlier + (key_span < query_span).astype(jnp.int32)

        def step(pair, carry):
            update([list_ref[2 * pair], list_ref[2 * pair + 1]], False)
            return carry

        lax.fori_loop(0, earlier // 2, step, 0)

        @pl.when(earlier % 2 == 1)
        def _():
            update([list_ref[earlier - 1]], False)

        if away == 0:
            update([0], True)

        total = jnp.maximum(sum_ref[...], 1.0)
        outs[number][:HD, :] = (acc_ref[...] / total).astype(jnp.bfloat16)
        level = max_ref[...] * SCALE_LOG2 + jnp.log2(total)
        high = level.astype(jnp.bfloat16).astype(jnp.float32)
        middle = (level - high).astype(jnp.bfloat16).astype(jnp.float32)
        low = level - high - middle
        row = lax.broadcasted_iota(jnp.int32, (STATS, ROWS), 0)
        stats = jnp.where(row == 0, high, jnp.where(row == 1, middle, jnp.where(row == 2, low, 0.0)))
        outs[number][HD:, :] = stats.astype(jnp.bfloat16)


def attend(block_span, steps, queries, messages):
    part = jax.ShapeDtypeStruct((HD + STATS, ROWS), jnp.bfloat16)
    return pl.pallas_call(
        functools.partial(attend_kernel, steps),
        out_shape=(part,) * len(steps),
        in_specs=[SMEM] + [VMEM] * (len(steps) + NZ),
        out_specs=(VMEM,) * len(steps),
        scratch_shapes=[
            pltpu.VMEM((NZ, SPAN, 2 * HD), jnp.bfloat16),
            pltpu.VMEM((HD, ROWS), jnp.float32),
            pltpu.VMEM((1, ROWS), jnp.float32),
            pltpu.VMEM((1, ROWS), jnp.float32),
            pltpu.SMEM((NZ + 1,), jnp.int32),
        ],
        compiler_params=params(32),
        cost_estimate=cost(10 * len(steps)),
        name="attend",
    )(block_span, *queries, *messages)


def merge_kernel(*refs):
    parts, out_ref = refs[:NY], refs[NY]
    levels = []
    for part in parts:
        stats = part[HD:, :].astype(jnp.float32)
        levels.append(stats[0:1] + stats[1:2] + stats[2:3])
    top = levels[0]
    for level in levels[1:]:
        top = jnp.maximum(top, level)
    weights = [jnp.exp2(level - top) for level in levels]
    total = weights[0]
    for weight in weights[1:]:
        total = total + weight
    for head in range(GQ):
        lanes = slice(head * SPAN, (head + 1) * SPAN)
        context = jnp.zeros((HD, SPAN), jnp.float32)
        for part, weight in zip(parts, weights):
            context = context + part[:HD, lanes].astype(jnp.float32) * weight[:, lanes]
        context = context / total[:, lanes]
        out_ref[:, head * HD : (head + 1) * HD] = context.T.astype(jnp.bfloat16)


def merge(parts):
    return pl.pallas_call(
        merge_kernel,
        out_shape=jax.ShapeDtypeStruct((SPAN, GQ * HD), jnp.bfloat16),
        in_specs=[VMEM] * NY,
        out_specs=VMEM,
        compiler_params=params(16),
        cost_estimate=cost(4),
        name="merge",
    )(*parts)


def rotation(positions):
    half_dim = HD // 2
    inv_freq = ROPE_BASE ** (-(2 * jnp.arange(half_dim)).astype(jnp.float32) / HD)
    angles = positions.astype(jnp.float32)[:, None] * inv_freq[None, :]
    cosine = jnp.cos(angles)
    sine = jnp.sin(angles)
    return jnp.concatenate([cosine, cosine], axis=1), jnp.concatenate([-sine, sine], axis=1)


def along_x(value, step):
    return lax.ppermute(value, "kvh", [(i, ((i // 2 + step) % 4) * 2 + i % 2) for i in range(8)])


def across(value):
    return lax.ppermute(value, "kvh", [(i, i ^ 1) for i in range(8)])


def along_y(value, step):
    return lax.ppermute(
        value, "ctx", [(i, ((i // NZ + step) % NY) * NZ + i % NZ) for i in range(N_CTX)]
    )


def along_z(value, step):
    return lax.ppermute(
        value, "ctx", [(i, (i // NZ) * NZ + (i % NZ + step) % NZ) for i in range(N_CTX)]
    )


def to_owners(value):
    return lax.all_to_all(value, "ctx", split_axis=0, concat_axis=0, tiled=True)


def shards(front_hidden, norm_gain, w_qkv, block_span, back_pages, page_dest):
    my_index = lax.axis_index("ctx")
    my_core = lax.axis_index("kvh") % 2

    first, second = bucket(page_dest, back_pages.reshape(OWN_CAP, PAGE_ROWS, HD))
    low, high = along_x(front_hidden, 1), along_x(front_hidden, -1)
    first, low, high = lax.optimization_barrier((first, low, high))
    first = to_owners(first)

    opposite = lax.ppermute(
        jnp.where(my_core == 0, low, high),
        "kvh",
        [(i, ((i // 2 + 1 - 2 * (i % 2)) % 4) * 2 + i % 2) for i in range(8)],
    )
    same = [front_hidden, low, high, opposite]
    other = [across(block) for block in same]

    my_span = jnp.sum(jnp.where(jnp.arange(N_CTX) == my_index, block_span, 0))
    cosine, sine = rotation(my_span * SPAN + jnp.arange(SPAN))
    gain = norm_gain.astype(jnp.float32).reshape(8, D // 8)
    query, cache, message = project(gain, cosine, sine, w_qkv, same + other)

    from_up = along_y(query, -1)
    queries = [query, along_y(query, 1), from_up, along_y(from_up, -1)]

    up, down = [message], [message]
    for _ in range(3):
        up.append(along_z(up[-1], 1))
        down.append(along_z(down[-1], -1))
    down.append(along_z(down[-1], -1))
    messages = up + down[1:]

    held = lax.optimization_barrier((second, *messages, *queries))
    second, messages, queries = held[0], held[1 : 1 + NZ], held[1 + NZ :]
    second = to_owners(second)

    back = []
    for group in ((3,), (1, 2), (0,)):
        parts = attend(
            block_span, [STEPS_Y[at] for at in group], [queries[at] for at in group], messages
        )
        for at, part in zip(group, parts):
            back.append(along_y(part, STEPS_Y[at]) if at else part)
    attn_out = merge(back)

    restored, page_count = place(first, second)
    return (
        attn_out,
        cache.reshape(SPAN, 1, 2 * HD),
        restored.reshape(back_pages.shape),
        page_count,
    )


def solution(mesh):
    placed = (
        P("ctx", "kvh"),
        P(),
        P(None, "kvh"),
        P(),
        P("ctx", "kvh", None, None, None),
        P("ctx"),
    )
    return jax.shard_map(
        shards,
        mesh=mesh,
        in_specs=placed,
        out_specs=(
            P("ctx", "kvh"),
            P("ctx", "kvh", None),
            P("ctx", "kvh", None, None, None),
            P("ctx"),
        ),
        check_vma=False,
    )
```

```python
import functools

import jax
import jax.numpy as jnp
from jax import lax
from jax.experimental import pallas as pl
from jax.experimental.pallas import tpu as pltpu
from jax.sharding import PartitionSpec as P

HD = 128
GQ = 4
SPAN = 256
SEND_CAP = 8
NY = 4
NZ = 8
N_CTX = NY * NZ
OWN_CAP = N_CTX * SEND_CAP
FIRST = 4
SECOND = SEND_CAP - FIRST
D = 4096
ROWS = GQ * SPAN
PAGE_ROWS = 32
ROPE_BASE = 500000.0
MASK_FILL = -1e30
SCALE_LOG2 = HD**-0.5 * 1.4426950408889634
MARK = 64.0
STATS = 16
STEPS_X = (0, 1, 3, 2)
STEPS_Y = (0, -1, 1, 2)
STEPS_Z = (0, -1, -2, -3, 1, 2, 3, 4)

VMEM = pl.BlockSpec(memory_space=pltpu.VMEM)
SMEM = pl.BlockSpec(memory_space=pltpu.SMEM)
HBM = pl.BlockSpec(memory_space=pltpu.HBM)


def params(mib):
    return pltpu.CompilerParams(vmem_limit_bytes=mib * 2**20)


def cost(mib):
    return pl.CostEstimate(flops=0, bytes_accessed=mib * 2**20, transcendentals=0)


def bucket_kernel(dest_hbm, pages_hbm, first_out, second_out, *refs):
    dest_ref, pages_ref, held_ref, count_ref, in_sems, sems = refs
    loads = [
        pltpu.make_async_copy(dest_hbm, dest_ref, in_sems.at[0]),
        pltpu.make_async_copy(pages_hbm, pages_ref, in_sems.at[1]),
    ]
    for load in loads:
        load.start()
    for owner in range(N_CTX + 1):
        count_ref[owner] = 0
    for load in loads:
        load.wait()

    def put(page, carry):
        owner = dest_ref[page]
        held = owner >= 0
        entry = jnp.where(held, owner, N_CTX)
        rank = count_ref[entry]
        count_ref[entry] = rank + 1
        held_ref[entry, jnp.where(held, rank, 0)] = pages_ref[page]
        return carry

    lax.fori_loop(0, OWN_CAP, put, 0, unroll=16)

    for entry in range(N_CTX):
        count = count_ref[entry]
        value = jnp.full((16, HD), MARK + count.astype(jnp.float32), jnp.float32)
        here = held_ref[entry, SEND_CAP - 1, 0:16, :]
        marked = jnp.where(count < SEND_CAP, value.astype(jnp.bfloat16), here)
        held_ref[entry, SEND_CAP - 1, 0:16, :] = marked
    buckets = held_ref.at[pl.ds(0, N_CTX)]
    copies = [
        pltpu.make_async_copy(buckets.at[:, pl.ds(0, FIRST)], first_out, sems.at[0]),
        pltpu.make_async_copy(buckets.at[:, pl.ds(FIRST, SECOND)], second_out, sems.at[1]),
    ]
    for copy in copies:
        copy.start()
    for copy in copies:
        copy.wait()


def bucket(page_dest, pages):
    return pl.pallas_call(
        bucket_kernel,
        out_shape=tuple(
            jax.ShapeDtypeStruct((N_CTX, n, PAGE_ROWS, HD), jnp.bfloat16) for n in (FIRST, SECOND)
        ),
        in_specs=[HBM, HBM],
        out_specs=(HBM, HBM),
        scratch_shapes=[
            pltpu.SMEM((OWN_CAP,), jnp.int32),
            pltpu.VMEM((OWN_CAP, PAGE_ROWS, HD), jnp.bfloat16),
            pltpu.VMEM((N_CTX + 1, SEND_CAP, PAGE_ROWS, HD), jnp.bfloat16),
            pltpu.SMEM((N_CTX + 1,), jnp.int32),
            pltpu.SemaphoreType.DMA((2,)),
            pltpu.SemaphoreType.DMA((2,)),
        ],
        compiler_params=params(56),
        cost_estimate=cost(18),
        name="bucket",
    )(page_dest, pages)


def place_kernel(first_ref, second_ref, out_ref, total_ref, held_ref, placed_ref, sems):
    copies = [
        pltpu.make_async_copy(first_ref, held_ref.at[:, pl.ds(0, FIRST)], sems.at[0]),
        pltpu.make_async_copy(second_ref, held_ref.at[:, pl.ds(FIRST, SECOND)], sems.at[1]),
    ]
    for copy in copies:
        copy.start()
    for copy in copies:
        copy.wait()
    offset = jnp.int32(0)
    for store in range(N_CTX):
        last = held_ref[store, SEND_CAP - 1, 0:16, :].astype(jnp.float32)
        top = jnp.max(last)
        count = jnp.where(top > MARK / 2, (top - MARK).astype(jnp.int32), SEND_CAP)
        for rank in range(SEND_CAP):
            placed_ref[offset + rank] = held_ref[store, rank]
        offset = offset + count
    total_ref[0] = offset

    def clear(page, carry):
        placed_ref[page] = jnp.zeros((PAGE_ROWS, HD), jnp.bfloat16)
        return carry

    lax.fori_loop(offset, OWN_CAP, clear, 0)
    copy = pltpu.make_async_copy(placed_ref.at[pl.ds(0, OWN_CAP)], out_ref, sems.at[0])
    copy.start()
    copy.wait()


def place(first, second):
    return pl.pallas_call(
        place_kernel,
        out_shape=(
            jax.ShapeDtypeStruct((OWN_CAP, PAGE_ROWS, HD), jnp.bfloat16),
            jax.ShapeDtypeStruct((1,), jnp.int32),
        ),
        in_specs=[HBM, HBM],
        out_specs=(HBM, SMEM),
        scratch_shapes=[
            pltpu.VMEM((N_CTX, SEND_CAP, PAGE_ROWS, HD), jnp.bfloat16),
            pltpu.VMEM((OWN_CAP + SEND_CAP, PAGE_ROWS, HD), jnp.bfloat16),
            pltpu.SemaphoreType.DMA((2,)),
        ],
        compiler_params=params(16),
        cost_estimate=cost(10),
        name="place",
    )(first, second)


def project_kernel(gain_ref, cos_ref, sin_ref, w_hbm, *refs):
    blocks = refs[:8]
    qt_ref, cache_ref, msg_ref, w_ref, normed_ref, sems = refs[8:]
    width = blocks[0].shape[1]
    loads = [
        pltpu.make_async_copy(
            w_hbm.at[pl.ds(at * width, width)], w_ref.at[pl.ds(at * width, width)], sems.at[at]
        )
        for at in range(8)
    ]
    for load in loads:
        load.start()
    squares = jnp.zeros((SPAN, HD), jnp.float32)
    for block in blocks:
        for at in range(0, width, HD):
            part = block[:, at : at + HD].astype(jnp.float32)
            squares = squares + part * part
    inverse = lax.rsqrt(jnp.sum(squares, axis=1, keepdims=True) * (1.0 / D) + 1e-05)
    my_kvh = lax.axis_index("kvh")
    my_x, my_core = my_kvh // 2, my_kvh % 2
    for number, block in enumerate(blocks):
        source = (my_x - STEPS_X[number % 4]) & 3
        index = source * 2 + (my_core if number < 4 else 1 - my_core)
        gain = gain_ref[pl.ds(index, 1), :]
        normed = block[...].astype(jnp.float32) * inverse * gain
        start = pl.multiple_of(index * width, width)
        normed_ref[:, pl.ds(start, width)] = normed.astype(jnp.bfloat16)
    projected = jnp.zeros((SPAN, w_ref.shape[1]), jnp.float32)
    for at in range(0, 8, 2):
        loads[at].wait()
        loads[at + 1].wait()
        part = slice(at * width, (at + 2) * width)
        projected += jnp.dot(normed_ref[:, part], w_ref[part], preferred_element_type=jnp.float32)
    cosine = cos_ref[...]
    sine = sin_ref[...]

    def rope(u):
        return u * cosine + pltpu.roll(u, HD // 2, 1) * sine

    for head in range(GQ):
        turned = rope(projected[:, head * HD : (head + 1) * HD])
        qt_ref[:, head * SPAN : (head + 1) * SPAN] = turned.T.astype(jnp.bfloat16)
    key = rope(projected[:, GQ * HD : (GQ + 1) * HD]).astype(jnp.bfloat16)
    value = projected[:, (GQ + 1) * HD :]
    cache_ref[:, :HD] = key
    cache_ref[:, HD:] = value.astype(jnp.bfloat16)
    msg_ref[:, :HD] = key
    for at in (0, HD):
        msg_ref[at : at + HD, HD:] = value[at : at + HD].T.astype(jnp.bfloat16)


def project(gain, cosine, sine, w_qkv, blocks):
    return pl.pallas_call(
        project_kernel,
        out_shape=(
            jax.ShapeDtypeStruct((HD, ROWS), jnp.bfloat16),
            jax.ShapeDtypeStruct((SPAN, 2 * HD), jnp.bfloat16),
            jax.ShapeDtypeStruct((SPAN, 2 * HD), jnp.bfloat16),
        ),
        in_specs=[VMEM] * 3 + [HBM] + [VMEM] * 8,
        out_specs=(VMEM, VMEM, VMEM),
        scratch_shapes=[
            pltpu.VMEM(w_qkv.shape, jnp.bfloat16),
            pltpu.VMEM((SPAN, D), jnp.bfloat16),
            pltpu.SemaphoreType.DMA((8,)),
        ],
        compiler_params=params(56),
        cost_estimate=cost(16),
        name="project",
    )(gain, cosine, sine, w_qkv, *blocks)


def attend_kernel(steps, span_ref, *refs):
    size = len(steps)
    queries = refs[:size]
    messages = refs[size : size + NZ]
    outs = refs[size + NZ : 2 * size + NZ]
    kv_ref, acc_ref, max_ref, sum_ref, list_ref = refs[2 * size + NZ :]
    my_index = lax.axis_index("ctx")
    my_y, my_z = my_index // NZ, my_index % NZ
    for number, message in enumerate(messages):
        kv_ref[number] = message[...]
    key_at = lax.broadcasted_iota(jnp.int32, (SPAN, SPAN), 0)
    query_at = lax.broadcasted_iota(jnp.int32, (SPAN, SPAN), 1)
    heads = [slice(head * SPAN, (head + 1) * SPAN) for head in range(GQ)]
    key_spans = [span_ref[my_y * NZ + ((my_z + step) & (NZ - 1))] for step in STEPS_Z]

    for number, away in enumerate(steps):
        query_ref = queries[number]
        query_span = span_ref[((my_y + away) & (NY - 1)) * NZ + my_z]
        acc_ref[...] = jnp.zeros_like(acc_ref)
        max_ref[...] = jnp.full_like(max_ref, MASK_FILL)
        sum_ref[...] = jnp.zeros_like(sum_ref)

        def update(parts, masked):
            keys, values = [], []
            for part in parts:
                keys.append(kv_ref[part, :, :HD])
                value = kv_ref[part, :, HD:]
                values += [value[:HD], value[HD:]]
            key = jnp.concatenate(keys, axis=0)
            value = jnp.concatenate(values, axis=1)
            scores = [
                jnp.dot(key, query_ref[:, lanes], preferred_element_type=jnp.float32)
                for lanes in heads
            ]
            if masked:
                scores = [jnp.where(key_at <= query_at, score, MASK_FILL) for score in scores]
            old = [max_ref[:, lanes] for lanes in heads]
            new = [
                jnp.maximum(top, jnp.max(score, axis=0, keepdims=True))
                for top, score in zip(old, scores)
            ]
            weights = [jnp.exp2((score - top) * SCALE_LOG2) for score, top in zip(scores, new)]
            fades = [jnp.exp2((before - top) * SCALE_LOG2) for before, top in zip(old, new)]
            products = [
                jnp.dot(value, weight.astype(jnp.bfloat16), preferred_element_type=jnp.float32)
                for weight in weights
            ]
            for head, lanes in enumerate(heads):
                total = jnp.sum(weights[head], axis=0, keepdims=True)
                sum_ref[:, lanes] = sum_ref[:, lanes] * fades[head] + total
                acc_ref[:, lanes] = acc_ref[:, lanes] * fades[head] + products[head]
                max_ref[:, lanes] = new[head]

        earlier = jnp.int32(0)
        for part, key_span in enumerate(key_spans):
            list_ref[earlier] = part
            earlier = earlier + (key_span < query_span).astype(jnp.int32)

        def step(group, carry):
            update([list_ref[4 * group + at] for at in range(4)], False)
            return carry

        lax.fori_loop(0, earlier // 4, step, 0)
        rest = earlier % 4

        @pl.when(rest >= 2)
        def _():
            update([list_ref[earlier - rest + at] for at in range(2)], False)

        @pl.when(rest % 2 == 1)
        def _():
            update([list_ref[earlier - 1]], False)

        if away == 0:
            update([0], True)

        total = jnp.maximum(sum_ref[...], 1.0)
        outs[number][:HD, :] = (acc_ref[...] / total).astype(jnp.bfloat16)
        level = max_ref[...] * SCALE_LOG2 + jnp.log2(total)
        high = level.astype(jnp.bfloat16).astype(jnp.float32)
        middle = (level - high).astype(jnp.bfloat16).astype(jnp.float32)
        low = level - high - middle
        row = lax.broadcasted_iota(jnp.int32, (STATS, ROWS), 0)
        stats = jnp.where(row == 0, high, jnp.where(row == 1, middle, jnp.where(row == 2, low, 0.0)))
        outs[number][HD:, :] = stats.astype(jnp.bfloat16)


def attend(block_span, steps, queries, messages):
    part = jax.ShapeDtypeStruct((HD + STATS, ROWS), jnp.bfloat16)
    return pl.pallas_call(
        functools.partial(attend_kernel, steps),
        out_shape=(part,) * len(steps),
        in_specs=[SMEM] + [VMEM] * (len(steps) + NZ),
        out_specs=(VMEM,) * len(steps),
        scratch_shapes=[
            pltpu.VMEM((NZ, SPAN, 2 * HD), jnp.bfloat16),
            pltpu.VMEM((HD, ROWS), jnp.float32),
            pltpu.VMEM((1, ROWS), jnp.float32),
            pltpu.VMEM((1, ROWS), jnp.float32),
            pltpu.SMEM((NZ + 1,), jnp.int32),
        ],
        compiler_params=params(32),
        cost_estimate=cost(10 * len(steps)),
        name="attend",
    )(block_span, *queries, *messages)


def merge_kernel(*refs):
    parts, out_ref = refs[:NY], refs[NY]
    levels = []
    for part in parts:
        stats = part[HD:, :].astype(jnp.float32)
        levels.append(stats[0:1] + stats[1:2] + stats[2:3])
    top = levels[0]
    for level in levels[1:]:
        top = jnp.maximum(top, level)
    weights = [jnp.exp2(level - top) for level in levels]
    total = weights[0]
    for weight in weights[1:]:
        total = total + weight
    for head in range(GQ):
        lanes = slice(head * SPAN, (head + 1) * SPAN)
        context = jnp.zeros((HD, SPAN), jnp.float32)
        for part, weight in zip(parts, weights):
            context = context + part[:HD, lanes].astype(jnp.float32) * weight[:, lanes]
        context = context / total[:, lanes]
        out_ref[:, head * HD : (head + 1) * HD] = context.T.astype(jnp.bfloat16)


def merge(parts):
    return pl.pallas_call(
        merge_kernel,
        out_shape=jax.ShapeDtypeStruct((SPAN, GQ * HD), jnp.bfloat16),
        in_specs=[VMEM] * NY,
        out_specs=VMEM,
        compiler_params=params(16),
        cost_estimate=cost(4),
        name="merge",
    )(*parts)


def rotation(positions):
    half_dim = HD // 2
    lane = jnp.arange(HD)
    inv_freq = ROPE_BASE ** (-(2 * (lane % half_dim)).astype(jnp.float32) / HD)
    angles = positions.astype(jnp.float32)[:, None] * inv_freq[None, :]
    sine = jnp.sin(angles)
    return jnp.cos(angles), jnp.where(lane[None, :] < half_dim, -sine, sine)


def along_x(value, step):
    return lax.ppermute(value, "kvh", [(i, ((i // 2 + step) % 4) * 2 + i % 2) for i in range(8)])


def across(value):
    return lax.ppermute(value, "kvh", [(i, i ^ 1) for i in range(8)])


def along_y(value, step):
    return lax.ppermute(
        value, "ctx", [(i, ((i // NZ + step) % NY) * NZ + i % NZ) for i in range(N_CTX)]
    )


def along_z(value, step):
    return lax.ppermute(
        value, "ctx", [(i, (i // NZ) * NZ + (i % NZ + step) % NZ) for i in range(N_CTX)]
    )


def to_owners(value):
    return lax.all_to_all(value, "ctx", split_axis=0, concat_axis=0, tiled=True)


def shards(front_hidden, norm_gain, w_qkv, block_span, back_pages, page_dest):
    my_index = lax.axis_index("ctx")

    first, second = bucket(page_dest, back_pages.reshape(OWN_CAP, PAGE_ROWS, HD))
    first = to_owners(first)

    my_span = jnp.sum(jnp.where(jnp.arange(N_CTX) == my_index, block_span, 0))
    cosine, sine = rotation(my_span * SPAN + jnp.arange(SPAN))
    gain = norm_gain.astype(jnp.float32).reshape(8, D // 8)

    same = [front_hidden] + [along_x(front_hidden, step) for step in STEPS_X[1:]]
    held = lax.optimization_barrier((same[3], cosine, sine, gain))
    same[3], cosine, sine, gain = held
    other = [across(block) for block in same]
    query, cache, message = project(gain, cosine, sine, w_qkv, same + other)

    from_up = along_y(query, -1)
    queries = [query, along_y(query, 1), from_up, along_y(from_up, -1)]

    up, down = [message], [message]
    for _ in range(3):
        up.append(along_z(up[-1], 1))
        down.append(along_z(down[-1], -1))
    down.append(along_z(down[-1], -1))
    messages = up + down[1:]

    held = lax.optimization_barrier((second, *messages, *queries))
    second, messages, queries = held[0], held[1 : 1 + NZ], held[1 + NZ :]
    second = to_owners(second)

    back = []
    for group in ((3,), (1, 2), (0,)):
        parts = attend(
            block_span, [STEPS_Y[at] for at in group], [queries[at] for at in group], messages
        )
        for at, part in zip(group, parts):
            back.append(along_y(part, STEPS_Y[at]) if at else part)
    attn_out = merge(back)

    restored, page_count = place(first, second)
    return (
        attn_out,
        cache.reshape(SPAN, 1, 2 * HD),
        restored.reshape(back_pages.shape),
        page_count,
    )


def solution(mesh):
    placed = (
        P("ctx", "kvh"),
        P(),
        P(None, "kvh"),
        P(),
        P("ctx", "kvh", None, None, None),
        P("ctx"),
    )
    return jax.shard_map(
        shards,
        mesh=mesh,
        in_specs=placed,
        out_specs=(
            P("ctx", "kvh"),
            P("ctx", "kvh", None),
            P("ctx", "kvh", None, None, None),
            P("ctx"),
        ),
        check_vma=False,
    )
```

```python
import functools

import jax
import jax.numpy as jnp
from jax import lax
from jax.experimental import pallas as pl
from jax.experimental.pallas import tpu as pltpu
from jax.sharding import PartitionSpec as P

HD = 128
GQ = 4
SPAN = 256
SEND_CAP = 8
NY = 4
NZ = 8
N_CTX = NY * NZ
OWN_CAP = N_CTX * SEND_CAP
FIRST = 4
SECOND = SEND_CAP - FIRST
D = 4096
ROWS = GQ * SPAN
PAGE_ROWS = 32
ROPE_BASE = 500000.0
MASK_FILL = -1e30
SCALE_LOG2 = HD**-0.5 * 1.4426950408889634
MARK = 64.0
STATS = 16
STEPS_X = (0, 1, 3, 2)
STEPS_Y = (0, -1, 1, 2)
STEPS_Z = (0, -1, -2, -3, 1, 2, 3, 4)

VMEM = pl.BlockSpec(memory_space=pltpu.VMEM)
SMEM = pl.BlockSpec(memory_space=pltpu.SMEM)
HBM = pl.BlockSpec(memory_space=pltpu.HBM)


def params(mib):
    return pltpu.CompilerParams(vmem_limit_bytes=mib * 2**20)


def cost(mib):
    return pl.CostEstimate(flops=0, bytes_accessed=mib * 2**20, transcendentals=0)


def bucket_kernel(dest_hbm, pages_hbm, first_out, second_out, *refs):
    dest_ref, pages_ref, held_ref, count_ref, in_sems, sems = refs
    loads = [
        pltpu.make_async_copy(dest_hbm, dest_ref, in_sems.at[0]),
        pltpu.make_async_copy(pages_hbm, pages_ref, in_sems.at[1]),
    ]
    for load in loads:
        load.start()
    for owner in range(N_CTX + 1):
        count_ref[owner] = 0
    for load in loads:
        load.wait()

    def put(page, carry):
        owner = dest_ref[page]
        held = owner >= 0
        entry = jnp.where(held, owner, N_CTX)
        rank = count_ref[entry]
        count_ref[entry] = rank + 1
        held_ref[entry, jnp.where(held, rank, 0)] = pages_ref[page]
        return carry

    lax.fori_loop(0, OWN_CAP, put, 0, unroll=16)

    for entry in range(N_CTX):
        count = count_ref[entry]
        value = jnp.full((16, HD), MARK + count.astype(jnp.float32), jnp.float32)
        here = held_ref[entry, SEND_CAP - 1, 0:16, :]
        marked = jnp.where(count < SEND_CAP, value.astype(jnp.bfloat16), here)
        held_ref[entry, SEND_CAP - 1, 0:16, :] = marked
    buckets = held_ref.at[pl.ds(0, N_CTX)]
    copies = [
        pltpu.make_async_copy(buckets.at[:, pl.ds(0, FIRST)], first_out, sems.at[0]),
        pltpu.make_async_copy(buckets.at[:, pl.ds(FIRST, SECOND)], second_out, sems.at[1]),
    ]
    for copy in copies:
        copy.start()
    for copy in copies:
        copy.wait()


def bucket(page_dest, pages):
    return pl.pallas_call(
        bucket_kernel,
        out_shape=tuple(
            jax.ShapeDtypeStruct((N_CTX, n, PAGE_ROWS, HD), jnp.bfloat16) for n in (FIRST, SECOND)
        ),
        in_specs=[HBM, HBM],
        out_specs=(HBM, HBM),
        scratch_shapes=[
            pltpu.SMEM((OWN_CAP,), jnp.int32),
            pltpu.VMEM((OWN_CAP, PAGE_ROWS, HD), jnp.bfloat16),
            pltpu.VMEM((N_CTX + 1, SEND_CAP, PAGE_ROWS, HD), jnp.bfloat16),
            pltpu.SMEM((N_CTX + 1,), jnp.int32),
            pltpu.SemaphoreType.DMA((2,)),
            pltpu.SemaphoreType.DMA((2,)),
        ],
        compiler_params=params(56),
        cost_estimate=cost(18),
        name="bucket",
    )(page_dest, pages)


def place_kernel(first_ref, second_ref, out_ref, total_ref, held_ref, placed_ref, sems):
    copies = [
        pltpu.make_async_copy(first_ref, held_ref.at[:, pl.ds(0, FIRST)], sems.at[0]),
        pltpu.make_async_copy(second_ref, held_ref.at[:, pl.ds(FIRST, SECOND)], sems.at[1]),
    ]
    for copy in copies:
        copy.start()
    for copy in copies:
        copy.wait()
    offset = jnp.int32(0)
    for store in range(N_CTX):
        last = held_ref[store, SEND_CAP - 1, 0:16, :].astype(jnp.float32)
        top = jnp.max(last)
        count = jnp.where(top > MARK / 2, (top - MARK).astype(jnp.int32), SEND_CAP)
        for rank in range(SEND_CAP):
            placed_ref[offset + rank] = held_ref[store, rank]
        offset = offset + count
    total_ref[0] = offset

    def clear(page, carry):
        placed_ref[page] = jnp.zeros((PAGE_ROWS, HD), jnp.bfloat16)
        return carry

    lax.fori_loop(offset, OWN_CAP, clear, 0)
    copy = pltpu.make_async_copy(placed_ref.at[pl.ds(0, OWN_CAP)], out_ref, sems.at[0])
    copy.start()
    copy.wait()


def place(first, second):
    return pl.pallas_call(
        place_kernel,
        out_shape=(
            jax.ShapeDtypeStruct((OWN_CAP, PAGE_ROWS, HD), jnp.bfloat16),
            jax.ShapeDtypeStruct((1,), jnp.int32),
        ),
        in_specs=[HBM, HBM],
        out_specs=(HBM, SMEM),
        scratch_shapes=[
            pltpu.VMEM((N_CTX, SEND_CAP, PAGE_ROWS, HD), jnp.bfloat16),
            pltpu.VMEM((OWN_CAP + SEND_CAP, PAGE_ROWS, HD), jnp.bfloat16),
            pltpu.SemaphoreType.DMA((2,)),
        ],
        compiler_params=params(16),
        cost_estimate=cost(10),
        name="place",
    )(first, second)


def project_kernel(gain_ref, cos_ref, sin_ref, w_hbm, *refs):
    blocks = refs[:8]
    qt_ref, cache_ref, msg_ref, w_ref, normed_ref, sems = refs[8:]
    width = blocks[0].shape[1]
    loads = [
        pltpu.make_async_copy(
            w_hbm.at[pl.ds(at * width, width)], w_ref.at[pl.ds(at * width, width)], sems.at[at]
        )
        for at in range(8)
    ]
    for load in loads:
        load.start()
    squares = jnp.zeros((SPAN, HD), jnp.float32)
    for block in blocks:
        for at in range(0, width, HD):
            part = block[:, at : at + HD].astype(jnp.float32)
            squares = squares + part * part
    inverse = lax.rsqrt(jnp.sum(squares, axis=1, keepdims=True) * (1.0 / D) + 1e-05)
    my_kvh = lax.axis_index("kvh")
    my_x, my_core = my_kvh // 2, my_kvh % 2
    for number, block in enumerate(blocks):
        source = (my_x - STEPS_X[number % 4]) & 3
        index = source * 2 + (my_core if number < 4 else 1 - my_core)
        gain = gain_ref[pl.ds(index, 1), :]
        normed = block[...].astype(jnp.float32) * inverse * gain
        start = pl.multiple_of(index * width, width)
        normed_ref[:, pl.ds(start, width)] = normed.astype(jnp.bfloat16)
    projected = jnp.zeros((SPAN, w_ref.shape[1]), jnp.float32)
    for at in range(0, 8, 2):
        loads[at].wait()
        loads[at + 1].wait()
        part = slice(at * width, (at + 2) * width)
        projected += jnp.dot(normed_ref[:, part], w_ref[part], preferred_element_type=jnp.float32)
    cosine = cos_ref[...]
    sine = sin_ref[...]

    def rope(u):
        return u * cosine + pltpu.roll(u, HD // 2, 1) * sine

    for head in range(GQ):
        turned = rope(projected[:, head * HD : (head + 1) * HD])
        qt_ref[:, head * SPAN : (head + 1) * SPAN] = turned.T.astype(jnp.bfloat16)
    key = rope(projected[:, GQ * HD : (GQ + 1) * HD]).astype(jnp.bfloat16)
    value = projected[:, (GQ + 1) * HD :]
    cache_ref[:, :HD] = key
    cache_ref[:, HD:] = value.astype(jnp.bfloat16)
    msg_ref[:, :HD] = key
    for at in (0, HD):
        msg_ref[at : at + HD, HD:] = value[at : at + HD].T.astype(jnp.bfloat16)


def project(gain, cosine, sine, w_qkv, blocks):
    return pl.pallas_call(
        project_kernel,
        out_shape=(
            jax.ShapeDtypeStruct((HD, ROWS), jnp.bfloat16),
            jax.ShapeDtypeStruct((SPAN, 2 * HD), jnp.bfloat16),
            jax.ShapeDtypeStruct((SPAN, 2 * HD), jnp.bfloat16),
        ),
        in_specs=[VMEM] * 3 + [HBM] + [VMEM] * 8,
        out_specs=(VMEM, VMEM, VMEM),
        scratch_shapes=[
            pltpu.VMEM(w_qkv.shape, jnp.bfloat16),
            pltpu.VMEM((SPAN, D), jnp.bfloat16),
            pltpu.SemaphoreType.DMA((8,)),
        ],
        compiler_params=params(50),
        cost_estimate=cost(16),
        name="project",
    )(gain, cosine, sine, w_qkv, *blocks)


def attend_kernel(steps, span_ref, *refs):
    size = len(steps)
    queries = refs[:size]
    messages = refs[size : size + NZ]
    outs = refs[size + NZ : 2 * size + NZ]
    kv_ref, acc_ref, max_ref, sum_ref, list_ref = refs[2 * size + NZ :]
    my_index = lax.axis_index("ctx")
    my_y, my_z = my_index // NZ, my_index % NZ
    for number, message in enumerate(messages):
        kv_ref[number] = message[...]
    key_at = lax.broadcasted_iota(jnp.int32, (SPAN, SPAN), 0)
    query_at = lax.broadcasted_iota(jnp.int32, (SPAN, SPAN), 1)
    heads = [slice(head * SPAN, (head + 1) * SPAN) for head in range(GQ)]
    key_spans = [span_ref[my_y * NZ + ((my_z + step) & (NZ - 1))] for step in STEPS_Z]

    for number, away in enumerate(steps):
        query_ref = queries[number]
        query_span = span_ref[((my_y + away) & (NY - 1)) * NZ + my_z]
        acc_ref[...] = jnp.zeros_like(acc_ref)
        max_ref[...] = jnp.full_like(max_ref, MASK_FILL)
        sum_ref[...] = jnp.zeros_like(sum_ref)

        def update(parts, masked):
            keys, values = [], []
            for part in parts:
                keys.append(kv_ref[part, :, :HD])
                value = kv_ref[part, :, HD:]
                values += [value[:HD], value[HD:]]
            key = jnp.concatenate(keys, axis=0)
            value = jnp.concatenate(values, axis=1)
            scores = [
                jnp.dot(key, query_ref[:, lanes], preferred_element_type=jnp.float32)
                for lanes in heads
            ]
            if masked:
                scores = [jnp.where(key_at <= query_at, score, MASK_FILL) for score in scores]
            old = [max_ref[:, lanes] for lanes in heads]
            new = [
                jnp.maximum(top, jnp.max(score, axis=0, keepdims=True))
                for top, score in zip(old, scores)
            ]
            weights = [jnp.exp2((score - top) * SCALE_LOG2) for score, top in zip(scores, new)]
            fades = [jnp.exp2((before - top) * SCALE_LOG2) for before, top in zip(old, new)]
            products = [
                jnp.dot(value, weight.astype(jnp.bfloat16), preferred_element_type=jnp.float32)
                for weight in weights
            ]
            for head, lanes in enumerate(heads):
                total = jnp.sum(weights[head], axis=0, keepdims=True)
                sum_ref[:, lanes] = sum_ref[:, lanes] * fades[head] + total
                acc_ref[:, lanes] = acc_ref[:, lanes] * fades[head] + products[head]
                max_ref[:, lanes] = new[head]

        earlier = jnp.int32(0)
        for part, key_span in enumerate(key_spans):
            list_ref[earlier] = part
            earlier = earlier + (key_span < query_span).astype(jnp.int32)

        def step(group, carry):
            update([list_ref[4 * group + at] for at in range(4)], False)
            return carry

        lax.fori_loop(0, earlier // 4, step, 0)
        rest = earlier % 4

        @pl.when(rest >= 2)
        def _():
            update([list_ref[earlier - rest + at] for at in range(2)], False)

        @pl.when(rest % 2 == 1)
        def _():
            update([list_ref[earlier - 1]], False)

        if away == 0:
            update([0], True)

        total = jnp.maximum(sum_ref[...], 1.0)
        outs[number][:HD, :] = (acc_ref[...] / total).astype(jnp.bfloat16)
        level = max_ref[...] * SCALE_LOG2 + jnp.log2(total)
        high = level.astype(jnp.bfloat16).astype(jnp.float32)
        middle = (level - high).astype(jnp.bfloat16).astype(jnp.float32)
        low = level - high - middle
        row = lax.broadcasted_iota(jnp.int32, (STATS, ROWS), 0)
        stats = jnp.where(row == 0, high, jnp.where(row == 1, middle, jnp.where(row == 2, low, 0.0)))
        outs[number][HD:, :] = stats.astype(jnp.bfloat16)


def attend(block_span, steps, queries, messages):
    part = jax.ShapeDtypeStruct((HD + STATS, ROWS), jnp.bfloat16)
    return pl.pallas_call(
        functools.partial(attend_kernel, steps),
        out_shape=(part,) * len(steps),
        in_specs=[SMEM] + [VMEM] * (len(steps) + NZ),
        out_specs=(VMEM,) * len(steps),
        scratch_shapes=[
            pltpu.VMEM((NZ, SPAN, 2 * HD), jnp.bfloat16),
            pltpu.VMEM((HD, ROWS), jnp.float32),
            pltpu.VMEM((1, ROWS), jnp.float32),
            pltpu.VMEM((1, ROWS), jnp.float32),
            pltpu.SMEM((NZ + 1,), jnp.int32),
        ],
        compiler_params=params(32),
        cost_estimate=cost(10 * len(steps)),
        name="attend",
    )(block_span, *queries, *messages)


def merge_kernel(*refs):
    parts, out_ref = refs[:NY], refs[NY]
    levels = []
    for part in parts:
        stats = part[HD:, :].astype(jnp.float32)
        levels.append(stats[0:1] + stats[1:2] + stats[2:3])
    top = levels[0]
    for level in levels[1:]:
        top = jnp.maximum(top, level)
    weights = [jnp.exp2(level - top) for level in levels]
    total = weights[0]
    for weight in weights[1:]:
        total = total + weight
    for head in range(GQ):
        lanes = slice(head * SPAN, (head + 1) * SPAN)
        context = jnp.zeros((HD, SPAN), jnp.float32)
        for part, weight in zip(parts, weights):
            context = context + part[:HD, lanes].astype(jnp.float32) * weight[:, lanes]
        context = context / total[:, lanes]
        out_ref[:, head * HD : (head + 1) * HD] = context.T.astype(jnp.bfloat16)


def merge(parts):
    return pl.pallas_call(
        merge_kernel,
        out_shape=jax.ShapeDtypeStruct((SPAN, GQ * HD), jnp.bfloat16),
        in_specs=[VMEM] * NY,
        out_specs=VMEM,
        compiler_params=params(16),
        cost_estimate=cost(4),
        name="merge",
    )(*parts)


def rotation(positions):
    half_dim = HD // 2
    lane = jnp.arange(HD)
    inv_freq = ROPE_BASE ** (-(2 * (lane % half_dim)).astype(jnp.float32) / HD)
    angles = positions.astype(jnp.float32)[:, None] * inv_freq[None, :]
    sine = jnp.sin(angles)
    return jnp.cos(angles), jnp.where(lane[None, :] < half_dim, -sine, sine)


def along_x(value, step):
    return lax.ppermute(value, "kvh", [(i, ((i // 2 + step) % 4) * 2 + i % 2) for i in range(8)])


def across(value):
    return lax.ppermute(value, "kvh", [(i, i ^ 1) for i in range(8)])


def along_y(value, step):
    return lax.ppermute(
        value, "ctx", [(i, ((i // NZ + step) % NY) * NZ + i % NZ) for i in range(N_CTX)]
    )


def along_z(value, step):
    return lax.ppermute(
        value, "ctx", [(i, (i // NZ) * NZ + (i % NZ + step) % NZ) for i in range(N_CTX)]
    )


def to_owners(value):
    return lax.all_to_all(value, "ctx", split_axis=0, concat_axis=0, tiled=True)


def shards(front_hidden, norm_gain, w_qkv, block_span, back_pages, page_dest):
    my_index = lax.axis_index("ctx")

    first, second = bucket(page_dest, back_pages.reshape(OWN_CAP, PAGE_ROWS, HD))
    first = to_owners(first)

    my_span = jnp.sum(jnp.where(jnp.arange(N_CTX) == my_index, block_span, 0))
    cosine, sine = rotation(my_span * SPAN + jnp.arange(SPAN))
    gain = norm_gain.astype(jnp.float32).reshape(8, D // 8)

    same = [front_hidden] + [along_x(front_hidden, step) for step in STEPS_X[1:]]
    held = lax.optimization_barrier((same[3], cosine, sine, gain))
    same[3], cosine, sine, gain = held
    other = [across(block) for block in same]
    query, cache, message = project(gain, cosine, sine, w_qkv, same + other)

    from_up = along_y(query, -1)
    queries = [query, along_y(query, 1), from_up, along_y(from_up, -1)]

    up, down = [message], [message]
    for _ in range(3):
        up.append(along_z(up[-1], 1))
        down.append(along_z(down[-1], -1))
    down.append(along_z(down[-1], -1))
    messages = up + down[1:]

    held = lax.optimization_barrier((second, *messages, *queries))
    second, messages, queries = held[0], held[1 : 1 + NZ], held[1 + NZ :]
    second = to_owners(second)

    back = []
    for group in ((3,), (1, 2), (0,)):
        parts = attend(
            block_span, [STEPS_Y[at] for at in group], [queries[at] for at in group], messages
        )
        for at, part in zip(group, parts):
            back.append(along_y(part, STEPS_Y[at]) if at else part)
    attn_out = merge(back)

    restored, page_count = place(first, second)
    return (
        attn_out,
        cache.reshape(SPAN, 1, 2 * HD),
        restored.reshape(back_pages.shape),
        page_count,
    )


def solution(mesh):
    placed = (
        P("ctx", "kvh"),
        P(),
        P(None, "kvh"),
        P(),
        P("ctx", "kvh", None, None, None),
        P("ctx"),
    )
    return jax.shard_map(
        shards,
        mesh=mesh,
        in_specs=placed,
        out_specs=(
            P("ctx", "kvh"),
            P("ctx", "kvh", None),
            P("ctx", "kvh", None, None, None),
            P("ctx"),
        ),
        check_vma=False,
    )
```

```python
import functools

import jax
import jax.numpy as jnp
from jax import lax
from jax.experimental import pallas as pl
from jax.experimental.pallas import tpu as pltpu
from jax.sharding import PartitionSpec as P

HD = 128
GQ = 4
SPAN = 256
SEND_CAP = 8
NY = 4
NZ = 8
N_CTX = NY * NZ
OWN_CAP = N_CTX * SEND_CAP
FIRST = 4
SECOND = SEND_CAP - FIRST
D = 4096
ROWS = GQ * SPAN
PAGE_ROWS = 32
ROPE_BASE = 500000.0
MASK_FILL = -1e30
SCALE_LOG2 = HD**-0.5 * 1.4426950408889634
MARK = 64.0
STATS = 16
PARTS = 4
STEPS_X = (0, 1, 3, 2)
STEPS_Y = (0, -1, 1, 2)
STEPS_Z = (0, -1, -2, -3, 1, 2, 3, 4)

VMEM = pl.BlockSpec(memory_space=pltpu.VMEM)
SMEM = pl.BlockSpec(memory_space=pltpu.SMEM)
HBM = pl.BlockSpec(memory_space=pltpu.HBM)


def params(mib):
    return pltpu.CompilerParams(vmem_limit_bytes=mib * 2**20)


def cost(mib):
    return pl.CostEstimate(flops=0, bytes_accessed=mib * 2**20, transcendentals=0)


def bucket_kernel(dest_hbm, pages_hbm, first_out, second_out, *refs):
    dest_ref, pages_ref, held_ref, count_ref, in_sems, sems = refs
    size = OWN_CAP // PARTS
    loads = [pltpu.make_async_copy(dest_hbm, dest_ref, in_sems.at[PARTS])]
    for part in range(PARTS):
        rows = pl.ds(part * size, size)
        loads.append(
            pltpu.make_async_copy(pages_hbm.at[rows], pages_ref.at[rows], in_sems.at[part])
        )
    for load in loads:
        load.start()
    for owner in range(N_CTX + 1):
        count_ref[owner] = 0
    loads[0].wait()

    def put(page, carry):
        owner = dest_ref[page]
        held = owner >= 0
        entry = jnp.where(held, owner, N_CTX)
        rank = count_ref[entry]
        count_ref[entry] = rank + 1
        held_ref[entry, jnp.where(held, rank, 0)] = pages_ref[page]
        return carry

    for part in range(PARTS):
        loads[1 + part].wait()
        lax.fori_loop(part * size, (part + 1) * size, put, 0, unroll=16)
    buckets = held_ref.at[pl.ds(0, N_CTX)]
    copies = [
        pltpu.make_async_copy(buckets.at[:, pl.ds(0, FIRST)], first_out, sems.at[0]),
        pltpu.make_async_copy(buckets.at[:, pl.ds(FIRST, SECOND)], second_out, sems.at[1]),
    ]
    copies[0].start()

    for entry in range(N_CTX):
        count = count_ref[entry]
        value = jnp.full((16, HD), MARK + count.astype(jnp.float32), jnp.float32)
        here = held_ref[entry, SEND_CAP - 1, 0:16, :]
        marked = jnp.where(count < SEND_CAP, value.astype(jnp.bfloat16), here)
        held_ref[entry, SEND_CAP - 1, 0:16, :] = marked
    copies[1].start()
    for copy in copies:
        copy.wait()


def bucket(page_dest, pages):
    return pl.pallas_call(
        bucket_kernel,
        out_shape=tuple(
            jax.ShapeDtypeStruct((N_CTX, n, PAGE_ROWS, HD), jnp.bfloat16) for n in (FIRST, SECOND)
        ),
        in_specs=[HBM, HBM],
        out_specs=(HBM, HBM),
        scratch_shapes=[
            pltpu.SMEM((OWN_CAP,), jnp.int32),
            pltpu.VMEM((OWN_CAP, PAGE_ROWS, HD), jnp.bfloat16),
            pltpu.VMEM((N_CTX + 1, SEND_CAP, PAGE_ROWS, HD), jnp.bfloat16),
            pltpu.SMEM((N_CTX + 1,), jnp.int32),
            pltpu.SemaphoreType.DMA((PARTS + 1,)),
            pltpu.SemaphoreType.DMA((2,)),
        ],
        compiler_params=params(56),
        cost_estimate=cost(18),
        name="bucket",
    )(page_dest, pages)


def place_kernel(first_ref, second_ref, out_ref, total_ref, held_ref, placed_ref, sems):
    copies = [
        pltpu.make_async_copy(first_ref, held_ref.at[:, pl.ds(0, FIRST)], sems.at[0]),
        pltpu.make_async_copy(second_ref, held_ref.at[:, pl.ds(FIRST, SECOND)], sems.at[1]),
    ]
    for copy in copies:
        copy.start()
    for copy in copies:
        copy.wait()
    counts = []
    for store in range(N_CTX):
        last = held_ref[store, SEND_CAP - 1, 0:16, :].astype(jnp.float32)
        top = jnp.max(last)
        counts.append(jnp.where(top > MARK / 2, (top - MARK).astype(jnp.int32), SEND_CAP))
    offset = jnp.int32(0)
    for store, count in enumerate(counts):
        for rank in range(SEND_CAP):
            placed_ref[offset + rank] = held_ref[store, rank]
        offset = offset + count
    total_ref[0] = offset

    def clear(page, carry):
        placed_ref[page] = jnp.zeros((PAGE_ROWS, HD), jnp.bfloat16)
        return carry

    lax.fori_loop(offset, OWN_CAP, clear, 0)
    copy = pltpu.make_async_copy(placed_ref.at[pl.ds(0, OWN_CAP)], out_ref, sems.at[0])
    copy.start()
    copy.wait()


def place(first, second):
    return pl.pallas_call(
        place_kernel,
        out_shape=(
            jax.ShapeDtypeStruct((OWN_CAP, PAGE_ROWS, HD), jnp.bfloat16),
            jax.ShapeDtypeStruct((1,), jnp.int32),
        ),
        in_specs=[HBM, HBM],
        out_specs=(HBM, SMEM),
        scratch_shapes=[
            pltpu.VMEM((N_CTX, SEND_CAP, PAGE_ROWS, HD), jnp.bfloat16),
            pltpu.VMEM((OWN_CAP + SEND_CAP, PAGE_ROWS, HD), jnp.bfloat16),
            pltpu.SemaphoreType.DMA((2,)),
        ],
        compiler_params=params(16),
        cost_estimate=cost(10),
        name="place",
    )(first, second)


def project_kernel(gain_ref, cos_ref, sin_ref, w_hbm, *refs):
    blocks = refs[:8]
    qt_ref, cache_ref, msg_ref, w_ref, normed_ref, sems = refs[8:]
    width = blocks[0].shape[1]
    loads = [
        pltpu.make_async_copy(
            w_hbm.at[pl.ds(at * width, width)], w_ref.at[pl.ds(at * width, width)], sems.at[at]
        )
        for at in range(8)
    ]
    for load in loads:
        load.start()
    squares = jnp.zeros((SPAN, HD), jnp.float32)
    for block in blocks:
        for at in range(0, width, HD):
            part = block[:, at : at + HD].astype(jnp.float32)
            squares = squares + part * part
    inverse = lax.rsqrt(jnp.sum(squares, axis=1, keepdims=True) * (1.0 / D) + 1e-05)
    my_kvh = lax.axis_index("kvh")
    my_x, my_core = my_kvh // 2, my_kvh % 2
    for number, block in enumerate(blocks):
        source = (my_x - STEPS_X[number % 4]) & 3
        index = source * 2 + (my_core if number < 4 else 1 - my_core)
        gain = gain_ref[pl.ds(index, 1), :]
        normed = block[...].astype(jnp.float32) * inverse * gain
        start = pl.multiple_of(index * width, width)
        normed_ref[:, pl.ds(start, width)] = normed.astype(jnp.bfloat16)
    projected = jnp.zeros((SPAN, w_ref.shape[1]), jnp.float32)
    for at in range(0, 8, 2):
        loads[at].wait()
        loads[at + 1].wait()
        part = slice(at * width, (at + 2) * width)
        projected += jnp.dot(normed_ref[:, part], w_ref[part], preferred_element_type=jnp.float32)
    cosine = cos_ref[...]
    sine = sin_ref[...]

    def rope(u):
        return u * cosine + pltpu.roll(u, HD // 2, 1) * sine

    for head in range(GQ):
        turned = rope(projected[:, head * HD : (head + 1) * HD])
        qt_ref[:, head * SPAN : (head + 1) * SPAN] = turned.T.astype(jnp.bfloat16)
    key = rope(projected[:, GQ * HD : (GQ + 1) * HD]).astype(jnp.bfloat16)
    value = projected[:, (GQ + 1) * HD :]
    cache_ref[:, :HD] = key
    cache_ref[:, HD:] = value.astype(jnp.bfloat16)
    msg_ref[:, :HD] = key
    for at in (0, HD):
        msg_ref[at : at + HD, HD:] = value[at : at + HD].T.astype(jnp.bfloat16)


def project(gain, cosine, sine, w_qkv, blocks):
    return pl.pallas_call(
        project_kernel,
        out_shape=(
            jax.ShapeDtypeStruct((HD, ROWS), jnp.bfloat16),
            jax.ShapeDtypeStruct((SPAN, 2 * HD), jnp.bfloat16),
            jax.ShapeDtypeStruct((SPAN, 2 * HD), jnp.bfloat16),
        ),
        in_specs=[VMEM] * 3 + [HBM] + [VMEM] * 8,
        out_specs=(VMEM, VMEM, VMEM),
        scratch_shapes=[
            pltpu.VMEM(w_qkv.shape, jnp.bfloat16),
            pltpu.VMEM((SPAN, D), jnp.bfloat16),
            pltpu.SemaphoreType.DMA((8,)),
        ],
        compiler_params=params(50),
        cost_estimate=cost(16),
        name="project",
    )(gain, cosine, sine, w_qkv, *blocks)


def attend_kernel(steps, span_ref, *refs):
    size = len(steps)
    queries = refs[:size]
    messages = refs[size : size + NZ]
    outs = refs[size + NZ : 2 * size + NZ]
    kv_ref, acc_ref, max_ref, sum_ref, list_ref = refs[2 * size + NZ :]
    my_index = lax.axis_index("ctx")
    my_y, my_z = my_index // NZ, my_index % NZ
    for number, message in enumerate(messages):
        kv_ref[number] = message[...]
    key_at = lax.broadcasted_iota(jnp.int32, (SPAN, SPAN), 0)
    query_at = lax.broadcasted_iota(jnp.int32, (SPAN, SPAN), 1)
    heads = [slice(head * SPAN, (head + 1) * SPAN) for head in range(GQ)]
    key_spans = [span_ref[my_y * NZ + ((my_z + step) & (NZ - 1))] for step in STEPS_Z]

    for number, away in enumerate(steps):
        query_ref = queries[number]
        query_span = span_ref[((my_y + away) & (NY - 1)) * NZ + my_z]
        acc_ref[...] = jnp.zeros_like(acc_ref)
        max_ref[...] = jnp.full_like(max_ref, MASK_FILL)
        sum_ref[...] = jnp.zeros_like(sum_ref)

        def update(parts, masked):
            keys, values = [], []
            for part in parts:
                keys.append(kv_ref[part, :, :HD])
                value = kv_ref[part, :, HD:]
                values += [value[:HD], value[HD:]]
            key = jnp.concatenate(keys, axis=0)
            value = jnp.concatenate(values, axis=1)
            scores = [
                jnp.dot(key, query_ref[:, lanes], preferred_element_type=jnp.float32)
                for lanes in heads
            ]
            if masked:
                scores = [jnp.where(key_at <= query_at, score, MASK_FILL) for score in scores]
            old = [max_ref[:, lanes] for lanes in heads]
            new = [
                jnp.maximum(top, jnp.max(score, axis=0, keepdims=True))
                for top, score in zip(old, scores)
            ]
            weights = [jnp.exp2((score - top) * SCALE_LOG2) for score, top in zip(scores, new)]
            fades = [jnp.exp2((before - top) * SCALE_LOG2) for before, top in zip(old, new)]
            products = [
                jnp.dot(value, weight.astype(jnp.bfloat16), preferred_element_type=jnp.float32)
                for weight in weights
            ]
            for head, lanes in enumerate(heads):
                total = jnp.sum(weights[head], axis=0, keepdims=True)
                sum_ref[:, lanes] = sum_ref[:, lanes] * fades[head] + total
                acc_ref[:, lanes] = acc_ref[:, lanes] * fades[head] + products[head]
                max_ref[:, lanes] = new[head]

        earlier = jnp.int32(0)
        for part, key_span in enumerate(key_spans):
            list_ref[earlier] = part
            earlier = earlier + (key_span < query_span).astype(jnp.int32)

        def step(group, carry):
            update([list_ref[4 * group + at] for at in range(4)], False)
            return carry

        lax.fori_loop(0, earlier // 4, step, 0)
        rest = earlier % 4

        @pl.when(rest >= 2)
        def _():
            update([list_ref[earlier - rest + at] for at in range(2)], False)

        @pl.when(rest % 2 == 1)
        def _():
            update([list_ref[earlier - 1]], False)

        if away == 0:
            update([0], True)

        total = jnp.maximum(sum_ref[...], 1.0)
        outs[number][:HD, :] = (acc_ref[...] / total).astype(jnp.bfloat16)
        level = max_ref[...] * SCALE_LOG2 + jnp.log2(total)
        high = level.astype(jnp.bfloat16).astype(jnp.float32)
        middle = (level - high).astype(jnp.bfloat16).astype(jnp.float32)
        low = level - high - middle
        row = lax.broadcasted_iota(jnp.int32, (STATS, ROWS), 0)
        stats = jnp.where(row == 0, high, jnp.where(row == 1, middle, jnp.where(row == 2, low, 0.0)))
        outs[number][HD:, :] = stats.astype(jnp.bfloat16)


def attend(block_span, steps, queries, messages):
    part = jax.ShapeDtypeStruct((HD + STATS, ROWS), jnp.bfloat16)
    return pl.pallas_call(
        functools.partial(attend_kernel, steps),
        out_shape=(part,) * len(steps),
        in_specs=[SMEM] + [VMEM] * (len(steps) + NZ),
        out_specs=(VMEM,) * len(steps),
        scratch_shapes=[
            pltpu.VMEM((NZ, SPAN, 2 * HD), jnp.bfloat16),
            pltpu.VMEM((HD, ROWS), jnp.float32),
            pltpu.VMEM((1, ROWS), jnp.float32),
            pltpu.VMEM((1, ROWS), jnp.float32),
            pltpu.SMEM((NZ + 1,), jnp.int32),
        ],
        compiler_params=params(32),
        cost_estimate=cost(10 * len(steps)),
        name="attend",
    )(block_span, *queries, *messages)


def merge_kernel(*refs):
    parts, out_ref = refs[:NY], refs[NY]
    levels = []
    for part in parts:
        stats = part[HD:, :].astype(jnp.float32)
        levels.append(stats[0:1] + stats[1:2] + stats[2:3])
    top = levels[0]
    for level in levels[1:]:
        top = jnp.maximum(top, level)
    weights = [jnp.exp2(level - top) for level in levels]
    total = weights[0]
    for weight in weights[1:]:
        total = total + weight
    for head in range(GQ):
        lanes = slice(head * SPAN, (head + 1) * SPAN)
        context = jnp.zeros((HD, SPAN), jnp.float32)
        for part, weight in zip(parts, weights):
            context = context + part[:HD, lanes].astype(jnp.float32) * weight[:, lanes]
        context = context / total[:, lanes]
        out_ref[:, head * HD : (head + 1) * HD] = context.T.astype(jnp.bfloat16)


def merge(parts):
    return pl.pallas_call(
        merge_kernel,
        out_shape=jax.ShapeDtypeStruct((SPAN, GQ * HD), jnp.bfloat16),
        in_specs=[VMEM] * NY,
        out_specs=VMEM,
        compiler_params=params(16),
        cost_estimate=cost(4),
        name="merge",
    )(*parts)


def rotation(positions):
    half_dim = HD // 2
    lane = jnp.arange(HD)
    inv_freq = ROPE_BASE ** (-(2 * (lane % half_dim)).astype(jnp.float32) / HD)
    angles = positions.astype(jnp.float32)[:, None] * inv_freq[None, :]
    sine = jnp.sin(angles)
    return jnp.cos(angles), jnp.where(lane[None, :] < half_dim, -sine, sine)


def along_x(value, step):
    return lax.ppermute(value, "kvh", [(i, ((i // 2 + step) % 4) * 2 + i % 2) for i in range(8)])


def across(value):
    return lax.ppermute(value, "kvh", [(i, i ^ 1) for i in range(8)])


def along_y(value, step):
    return lax.ppermute(
        value, "ctx", [(i, ((i // NZ + step) % NY) * NZ + i % NZ) for i in range(N_CTX)]
    )


def along_z(value, step):
    return lax.ppermute(
        value, "ctx", [(i, (i // NZ) * NZ + (i % NZ + step) % NZ) for i in range(N_CTX)]
    )


def to_owners(value):
    return lax.all_to_all(value, "ctx", split_axis=0, concat_axis=0, tiled=True)


def shards(front_hidden, norm_gain, w_qkv, block_span, back_pages, page_dest):
    my_index = lax.axis_index("ctx")

    first, second = bucket(page_dest, back_pages.reshape(OWN_CAP, PAGE_ROWS, HD))
    first = to_owners(first)

    my_span = jnp.sum(jnp.where(jnp.arange(N_CTX) == my_index, block_span, 0))
    cosine, sine = rotation(my_span * SPAN + jnp.arange(SPAN))
    gain = norm_gain.astype(jnp.float32).reshape(8, D // 8)

    same = [front_hidden] + [along_x(front_hidden, step) for step in STEPS_X[1:]]
    held = lax.optimization_barrier((same[3], cosine, sine, gain))
    same[3], cosine, sine, gain = held
    other = [across(block) for block in same]
    query, cache, message = project(gain, cosine, sine, w_qkv, same + other)

    from_up = along_y(query, -1)
    queries = [query, along_y(query, 1), from_up, along_y(from_up, -1)]

    up, down = [message], [message]
    for _ in range(3):
        up.append(along_z(up[-1], 1))
        down.append(along_z(down[-1], -1))
    down.append(along_z(down[-1], -1))
    messages = up + down[1:]

    held = lax.optimization_barrier((second, *messages, *queries))
    second, messages, queries = held[0], held[1 : 1 + NZ], held[1 + NZ :]
    second = to_owners(second)

    back = []
    for group in ((3,), (1, 2), (0,)):
        parts = attend(
            block_span, [STEPS_Y[at] for at in group], [queries[at] for at in group], messages
        )
        for at, part in zip(group, parts):
            back.append(along_y(part, STEPS_Y[at]) if at else part)
    attn_out = merge(back)

    restored, page_count = place(first, second)
    return (
        attn_out,
        cache.reshape(SPAN, 1, 2 * HD),
        restored.reshape(back_pages.shape),
        page_count,
    )


def solution(mesh):
    placed = (
        P("ctx", "kvh"),
        P(),
        P(None, "kvh"),
        P(),
        P("ctx", "kvh", None, None, None),
        P("ctx"),
    )
    return jax.shard_map(
        shards,
        mesh=mesh,
        in_specs=placed,
        out_specs=(
            P("ctx", "kvh"),
            P("ctx", "kvh", None),
            P("ctx", "kvh", None, None, None),
            P("ctx"),
        ),
        check_vma=False,
    )
```

```python
import functools

import jax
import jax.numpy as jnp
from jax import lax
from jax.experimental import pallas as pl
from jax.experimental.pallas import tpu as pltpu
from jax.sharding import PartitionSpec as P

HD = 128
GQ = 4
SPAN = 256
SEND_CAP = 8
NY = 4
NZ = 8
N_CTX = NY * NZ
OWN_CAP = N_CTX * SEND_CAP
FIRST = 4
SECOND = SEND_CAP - FIRST
D = 4096
ROWS = GQ * SPAN
PAGE_ROWS = 32
ROPE_BASE = 500000.0
MASK_FILL = -1e30
SCALE_LOG2 = HD**-0.5 * 1.4426950408889634
MARK = 64.0
STATS = 16
PARTS = 4
STEPS_X = (0, 1, 3, 2)
STEPS_Y = (0, -1, 1, 2)
STEPS_Z = (0, -1, -2, -3, 1, 2, 3, 4)

VMEM = pl.BlockSpec(memory_space=pltpu.VMEM)
SMEM = pl.BlockSpec(memory_space=pltpu.SMEM)
HBM = pl.BlockSpec(memory_space=pltpu.HBM)


def params(mib):
    return pltpu.CompilerParams(vmem_limit_bytes=mib * 2**20)


def cost(mib):
    return pl.CostEstimate(flops=0, bytes_accessed=mib * 2**20, transcendentals=0)


def bucket_kernel(dest_hbm, pages_hbm, first_out, second_out, *refs):
    dest_ref, pages_ref, held_ref, count_ref, in_sems, sems = refs
    size = OWN_CAP // PARTS
    loads = [pltpu.make_async_copy(dest_hbm, dest_ref, in_sems.at[PARTS])]
    for part in range(PARTS):
        rows = pl.ds(part * size, size)
        loads.append(
            pltpu.make_async_copy(pages_hbm.at[rows], pages_ref.at[rows], in_sems.at[part])
        )
    for load in loads:
        load.start()
    for owner in range(N_CTX + 1):
        count_ref[owner] = 0
    loads[0].wait()

    def put(page, carry):
        owner = dest_ref[page]
        held = owner >= 0
        entry = jnp.where(held, owner, N_CTX)
        rank = count_ref[entry]
        count_ref[entry] = rank + 1
        held_ref[entry, jnp.where(held, rank, 0)] = pages_ref[page]
        return carry

    for part in range(PARTS):
        loads[1 + part].wait()
        lax.fori_loop(part * size, (part + 1) * size, put, 0, unroll=16)
    buckets = held_ref.at[pl.ds(0, N_CTX)]
    copies = [
        pltpu.make_async_copy(buckets.at[:, pl.ds(0, FIRST)], first_out, sems.at[0]),
        pltpu.make_async_copy(buckets.at[:, pl.ds(FIRST, SECOND)], second_out, sems.at[1]),
    ]
    copies[0].start()

    for entry in range(N_CTX):
        count = count_ref[entry]
        value = jnp.full((16, HD), MARK + count.astype(jnp.float32), jnp.float32)
        here = held_ref[entry, SEND_CAP - 1, 0:16, :]
        marked = jnp.where(count < SEND_CAP, value.astype(jnp.bfloat16), here)
        held_ref[entry, SEND_CAP - 1, 0:16, :] = marked
    copies[1].start()
    for copy in copies:
        copy.wait()


def bucket(page_dest, pages):
    return pl.pallas_call(
        bucket_kernel,
        out_shape=tuple(
            jax.ShapeDtypeStruct((N_CTX, n, PAGE_ROWS, HD), jnp.bfloat16) for n in (FIRST, SECOND)
        ),
        in_specs=[HBM, HBM],
        out_specs=(HBM, HBM),
        scratch_shapes=[
            pltpu.SMEM((OWN_CAP,), jnp.int32),
            pltpu.VMEM((OWN_CAP, PAGE_ROWS, HD), jnp.bfloat16),
            pltpu.VMEM((N_CTX + 1, SEND_CAP, PAGE_ROWS, HD), jnp.bfloat16),
            pltpu.SMEM((N_CTX + 1,), jnp.int32),
            pltpu.SemaphoreType.DMA((PARTS + 1,)),
            pltpu.SemaphoreType.DMA((2,)),
        ],
        compiler_params=params(56),
        cost_estimate=cost(18),
        name="bucket",
    )(page_dest, pages)


def place_kernel(first_ref, second_ref, out_ref, total_ref, held_ref, placed_ref, sems):
    copies = [
        pltpu.make_async_copy(first_ref, held_ref.at[:, pl.ds(0, FIRST)], sems.at[0]),
        pltpu.make_async_copy(second_ref, held_ref.at[:, pl.ds(FIRST, SECOND)], sems.at[1]),
    ]
    for copy in copies:
        copy.start()
    for copy in copies:
        copy.wait()
    counts = []
    for store in range(N_CTX):
        last = held_ref[store, SEND_CAP - 1, 0:16, :].astype(jnp.float32)
        top = jnp.max(last)
        counts.append(jnp.where(top > MARK / 2, (top - MARK).astype(jnp.int32), SEND_CAP))
    offset = jnp.int32(0)
    for store, count in enumerate(counts):
        for rank in range(SEND_CAP):
            placed_ref[offset + rank] = held_ref[store, rank]
        offset = offset + count
    total_ref[0] = offset

    def clear(page, carry):
        placed_ref[page] = jnp.zeros((PAGE_ROWS, HD), jnp.bfloat16)
        return carry

    lax.fori_loop(offset, OWN_CAP, clear, 0)
    copy = pltpu.make_async_copy(placed_ref.at[pl.ds(0, OWN_CAP)], out_ref, sems.at[0])
    copy.start()
    copy.wait()


def place(first, second):
    return pl.pallas_call(
        place_kernel,
        out_shape=(
            jax.ShapeDtypeStruct((OWN_CAP, PAGE_ROWS, HD), jnp.bfloat16),
            jax.ShapeDtypeStruct((1,), jnp.int32),
        ),
        in_specs=[HBM, HBM],
        out_specs=(HBM, SMEM),
        scratch_shapes=[
            pltpu.VMEM((N_CTX, SEND_CAP, PAGE_ROWS, HD), jnp.bfloat16),
            pltpu.VMEM((OWN_CAP + SEND_CAP, PAGE_ROWS, HD), jnp.bfloat16),
            pltpu.SemaphoreType.DMA((2,)),
        ],
        compiler_params=params(16),
        cost_estimate=cost(10),
        name="place",
    )(first, second)


def project_kernel(gain_ref, cos_ref, sin_ref, w_hbm, *refs):
    blocks = refs[:8]
    qt_ref, cache_ref, msg_ref, w_ref, normed_ref, sems = refs[8:]
    width = blocks[0].shape[1]
    loads = [
        pltpu.make_async_copy(
            w_hbm.at[pl.ds(at * width, width)], w_ref.at[pl.ds(at * width, width)], sems.at[at]
        )
        for at in range(8)
    ]
    for load in loads:
        load.start()
    squares = jnp.zeros((SPAN, HD), jnp.float32)
    for block in blocks:
        for at in range(0, width, HD):
            part = block[:, at : at + HD].astype(jnp.float32)
            squares = squares + part * part
    inverse = lax.rsqrt(jnp.sum(squares, axis=1, keepdims=True) * (1.0 / D) + 1e-05)
    my_kvh = lax.axis_index("kvh")
    my_x, my_core = my_kvh // 2, my_kvh % 2
    for number, block in enumerate(blocks):
        source = (my_x - STEPS_X[number % 4]) & 3
        index = source * 2 + (my_core if number < 4 else 1 - my_core)
        gain = gain_ref[pl.ds(index, 1), :]
        normed = block[...].astype(jnp.float32) * inverse * gain
        start = pl.multiple_of(index * width, width)
        normed_ref[:, pl.ds(start, width)] = normed.astype(jnp.bfloat16)
    projected = jnp.zeros((SPAN, w_ref.shape[1]), jnp.float32)
    for at in range(0, 8, 2):
        loads[at].wait()
        loads[at + 1].wait()
        part = slice(at * width, (at + 2) * width)
        projected += jnp.dot(normed_ref[:, part], w_ref[part], preferred_element_type=jnp.float32)
    cosine = cos_ref[...]
    sine = sin_ref[...]

    def rope(u):
        return u * cosine + pltpu.roll(u, HD // 2, 1) * sine

    for head in range(GQ):
        turned = rope(projected[:, head * HD : (head + 1) * HD])
        qt_ref[:, head * SPAN : (head + 1) * SPAN] = turned.T.astype(jnp.bfloat16)
    key = rope(projected[:, GQ * HD : (GQ + 1) * HD]).astype(jnp.bfloat16)
    value = projected[:, (GQ + 1) * HD :]
    cache_ref[:, :HD] = key
    cache_ref[:, HD:] = value.astype(jnp.bfloat16)
    msg_ref[:, :HD] = key
    for at in (0, HD):
        msg_ref[at : at + HD, HD:] = value[at : at + HD].T.astype(jnp.bfloat16)


def project(gain, cosine, sine, w_qkv, blocks):
    return pl.pallas_call(
        project_kernel,
        out_shape=(
            jax.ShapeDtypeStruct((HD, ROWS), jnp.bfloat16),
            jax.ShapeDtypeStruct((SPAN, 2 * HD), jnp.bfloat16),
            jax.ShapeDtypeStruct((SPAN, 2 * HD), jnp.bfloat16),
        ),
        in_specs=[VMEM] * 3 + [HBM] + [VMEM] * 8,
        out_specs=(VMEM, VMEM, VMEM),
        scratch_shapes=[
            pltpu.VMEM(w_qkv.shape, jnp.bfloat16),
            pltpu.VMEM((SPAN, D), jnp.bfloat16),
            pltpu.SemaphoreType.DMA((8,)),
        ],
        compiler_params=params(50),
        cost_estimate=cost(16),
        name="project",
    )(gain, cosine, sine, w_qkv, *blocks)


def attend_kernel(steps, span_ref, *refs):
    size = len(steps)
    queries = refs[:size]
    messages = refs[size : size + NZ]
    outs = refs[size + NZ : 2 * size + NZ]
    kv_ref, acc_ref, max_ref, sum_ref, list_ref = refs[2 * size + NZ :]
    my_index = lax.axis_index("ctx")
    my_y, my_z = my_index // NZ, my_index % NZ
    for number, message in enumerate(messages):
        kv_ref[number] = message[...]
    key_at = lax.broadcasted_iota(jnp.int32, (SPAN, SPAN), 0)
    query_at = lax.broadcasted_iota(jnp.int32, (SPAN, SPAN), 1)
    heads = [slice(head * SPAN, (head + 1) * SPAN) for head in range(GQ)]
    key_spans = [span_ref[my_y * NZ + ((my_z + step) & (NZ - 1))] for step in STEPS_Z]

    for number, away in enumerate(steps):
        query_ref = queries[number]
        query_span = span_ref[((my_y + away) & (NY - 1)) * NZ + my_z]
        acc_ref[...] = jnp.zeros_like(acc_ref)
        max_ref[...] = jnp.full_like(max_ref, MASK_FILL)
        sum_ref[...] = jnp.zeros_like(sum_ref)

        def update(parts, masked):
            keys, values = [], []
            for part in parts:
                keys.append(kv_ref[part, :, :HD])
                value = kv_ref[part, :, HD:]
                values += [value[:HD], value[HD:]]
            key = jnp.concatenate(keys, axis=0)
            value = jnp.concatenate(values, axis=1)
            scores = [
                jnp.dot(key, query_ref[:, lanes], preferred_element_type=jnp.float32)
                for lanes in heads
            ]
            if masked:
                scores = [jnp.where(key_at <= query_at, score, MASK_FILL) for score in scores]
            old = [max_ref[:, lanes] for lanes in heads]
            new = [
                jnp.maximum(top, jnp.max(score, axis=0, keepdims=True))
                for top, score in zip(old, scores)
            ]
            weights = [jnp.exp2((score - top) * SCALE_LOG2) for score, top in zip(scores, new)]
            fades = [jnp.exp2((before - top) * SCALE_LOG2) for before, top in zip(old, new)]
            products = [
                jnp.dot(value, weight.astype(jnp.bfloat16), preferred_element_type=jnp.float32)
                for weight in weights
            ]
            for head, lanes in enumerate(heads):
                total = jnp.sum(weights[head], axis=0, keepdims=True)
                sum_ref[:, lanes] = sum_ref[:, lanes] * fades[head] + total
                acc_ref[:, lanes] = acc_ref[:, lanes] * fades[head] + products[head]
                max_ref[:, lanes] = new[head]

        earlier = jnp.int32(0)
        for part, key_span in enumerate(key_spans):
            list_ref[earlier] = part
            earlier = earlier + (key_span < query_span).astype(jnp.int32)

        def step(group, carry):
            update([list_ref[4 * group + at] for at in range(4)], False)
            return carry

        lax.fori_loop(0, earlier // 4, step, 0)
        rest = earlier % 4

        @pl.when(rest >= 2)
        def _():
            update([list_ref[earlier - rest + at] for at in range(2)], False)

        @pl.when(rest % 2 == 1)
        def _():
            update([list_ref[earlier - 1]], False)

        if away == 0:
            update([0], True)

        total = jnp.maximum(sum_ref[...], 1.0)
        outs[number][:HD, :] = (acc_ref[...] / total).astype(jnp.bfloat16)
        level = max_ref[...] * SCALE_LOG2 + jnp.log2(total)
        high = level.astype(jnp.bfloat16).astype(jnp.float32)
        middle = (level - high).astype(jnp.bfloat16).astype(jnp.float32)
        low = level - high - middle
        row = lax.broadcasted_iota(jnp.int32, (STATS, ROWS), 0)
        stats = jnp.where(row == 0, high, jnp.where(row == 1, middle, jnp.where(row == 2, low, 0.0)))
        outs[number][HD:, :] = stats.astype(jnp.bfloat16)


def attend(block_span, steps, queries, messages):
    part = jax.ShapeDtypeStruct((HD + STATS, ROWS), jnp.bfloat16)
    return pl.pallas_call(
        functools.partial(attend_kernel, steps),
        out_shape=(part,) * len(steps),
        in_specs=[SMEM] + [VMEM] * (len(steps) + NZ),
        out_specs=(VMEM,) * len(steps),
        scratch_shapes=[
            pltpu.VMEM((NZ, SPAN, 2 * HD), jnp.bfloat16),
            pltpu.VMEM((HD, ROWS), jnp.float32),
            pltpu.VMEM((1, ROWS), jnp.float32),
            pltpu.VMEM((1, ROWS), jnp.float32),
            pltpu.SMEM((NZ + 1,), jnp.int32),
        ],
        compiler_params=params(32),
        cost_estimate=cost(10 * len(steps)),
        name="attend",
    )(block_span, *queries, *messages)


def merge_kernel(*refs):
    parts, out_ref = refs[:NY], refs[NY]
    levels = []
    for part in parts:
        stats = part[HD:, :].astype(jnp.float32)
        levels.append(stats[0:1] + stats[1:2] + stats[2:3])
    top = levels[0]
    for level in levels[1:]:
        top = jnp.maximum(top, level)
    weights = [jnp.exp2(level - top) for level in levels]
    total = weights[0]
    for weight in weights[1:]:
        total = total + weight
    for head in range(GQ):
        lanes = slice(head * SPAN, (head + 1) * SPAN)
        context = jnp.zeros((HD, SPAN), jnp.float32)
        for part, weight in zip(parts, weights):
            context = context + part[:HD, lanes].astype(jnp.float32) * weight[:, lanes]
        context = context / total[:, lanes]
        out_ref[:, head * HD : (head + 1) * HD] = context.T.astype(jnp.bfloat16)


def merge(parts):
    return pl.pallas_call(
        merge_kernel,
        out_shape=jax.ShapeDtypeStruct((SPAN, GQ * HD), jnp.bfloat16),
        in_specs=[VMEM] * NY,
        out_specs=VMEM,
        compiler_params=params(16),
        cost_estimate=cost(4),
        name="merge",
    )(*parts)


def rotation(positions):
    half_dim = HD // 2
    lane = jnp.arange(HD)
    inv_freq = ROPE_BASE ** (-(2 * (lane % half_dim)).astype(jnp.float32) / HD)
    angles = positions.astype(jnp.float32)[:, None] * inv_freq[None, :]
    sine = jnp.sin(angles)
    return jnp.cos(angles), jnp.where(lane[None, :] < half_dim, -sine, sine)


def along_x(value, step):
    return lax.ppermute(value, "kvh", [(i, ((i // 2 + step) % 4) * 2 + i % 2) for i in range(8)])


def across(value):
    return lax.ppermute(value, "kvh", [(i, i ^ 1) for i in range(8)])


def along_y(value, step):
    return lax.ppermute(
        value, "ctx", [(i, ((i // NZ + step) % NY) * NZ + i % NZ) for i in range(N_CTX)]
    )


def along_z(value, step):
    return lax.ppermute(
        value, "ctx", [(i, (i // NZ) * NZ + (i % NZ + step) % NZ) for i in range(N_CTX)]
    )


def to_owners(value):
    return lax.all_to_all(value, "ctx", split_axis=0, concat_axis=0, tiled=True)


def shards(front_hidden, norm_gain, w_qkv, block_span, back_pages, page_dest):
    my_index = lax.axis_index("ctx")

    first, second = bucket(page_dest, back_pages.reshape(OWN_CAP, PAGE_ROWS, HD))
    first = to_owners(first)

    my_span = jnp.sum(jnp.where(jnp.arange(N_CTX) == my_index, block_span, 0))
    cosine, sine = rotation(my_span * SPAN + jnp.arange(SPAN))
    gain = norm_gain.astype(jnp.float32).reshape(8, D // 8)

    same = [front_hidden] + [along_x(front_hidden, step) for step in STEPS_X[1:]]
    held = lax.optimization_barrier((same[3], cosine, sine, gain))
    same[3], cosine, sine, gain = held
    other = [across(block) for block in same]
    query, cache, message = project(gain, cosine, sine, w_qkv, same + other)

    queries = [query] + [along_y(query, -step) for step in STEPS_Y[1:]]

    up, down = [message], [message]
    for _ in range(3):
        up.append(along_z(up[-1], 1))
        down.append(along_z(down[-1], -1))
    down.append(along_z(down[-1], -1))
    messages = up + down[1:]

    held = lax.optimization_barrier((second, *messages, *queries))
    second, messages, queries = held[0], held[1 : 1 + NZ], held[1 + NZ :]
    second = to_owners(second)

    back = []
    for group in ((3,), (1, 2), (0,)):
        parts = attend(
            block_span, [STEPS_Y[at] for at in group], [queries[at] for at in group], messages
        )
        for at, part in zip(group, parts):
            back.append(along_y(part, STEPS_Y[at]) if at else part)
    attn_out = merge(back)

    restored, page_count = place(first, second)
    return (
        attn_out,
        cache.reshape(SPAN, 1, 2 * HD),
        restored.reshape(back_pages.shape),
        page_count,
    )


def solution(mesh):
    placed = (
        P("ctx", "kvh"),
        P(),
        P(None, "kvh"),
        P(),
        P("ctx", "kvh", None, None, None),
        P("ctx"),
    )
    return jax.shard_map(
        shards,
        mesh=mesh,
        in_specs=placed,
        out_specs=(
            P("ctx", "kvh"),
            P("ctx", "kvh", None),
            P("ctx", "kvh", None, None, None),
            P("ctx"),
        ),
        check_vma=False,
    )
```
